32 devices in a mesh: wide: 8 (over z, y), narrow: 4 (over x, core).
Axes of the slice: x: 2, y: 2, z: 4, core: 2. Of those that a mesh axis runs over, the one named last changes fastest.
Arguments:
- frames: bfloat16 [65536, 256], P(('wide', 'narrow')), may hold values from -6 to 6
- segments: int32 [128, 512], P(('wide', 'narrow')), may hold values from 0 to 3, never falling along the last dimension, each value on 1 to 256 neighbouring positions
- out_grad: bfloat16 [65536, 256], P(('wide', 'narrow')), may hold values from -6 to 6
- attention_weights: float32 [4, 256, 256], P(None, ('wide', 'narrow')), may hold values from -0.9375 to 0.9375
- weight_in: float32 [256, 2048], P(('wide', 'narrow')), may hold values from -0.375 to 0.375
- weight_out: float32 [2048, 256], P(('wide', 'narrow')), may hold values from -0.125 to 0.125
- norm_gains: float32 [512], P(('wide', 'narrow')), may hold values from 0.5 to 1.5
- biases: float32 [3584], P(('wide', 'narrow')), may hold values from -1.2 to 1.2
- first_attention: float32 [4, 256, 256], P(None, ('wide', 'narrow')), may hold values from -51.2 to 51.2
- first_in: float32 [256, 2048], P(('wide', 'narrow')), may hold values from -51.2 to 51.2
- first_out: float32 [2048, 256], P(('wide', 'narrow')), may hold values from -51.2 to 51.2
- first_gains: float32 [512], P(('wide', 'narrow')), may hold values from -115.2 to 115.2
- first_biases: float32 [3584], P(('wide', 'narrow')), may hold values from -115.2 to 115.2
- second_attention: float32 [4, 256, 256], P(None, ('wide', 'narrow')), may hold values from 5.89824 to 23.59296
- second_in: float32 [256, 2048], P(('wide', 'narrow')), may hold values from 5.89824 to 23.59296
- second_out: float32 [2048, 256], P(('wide', 'narrow')), may hold values from 5.89824 to 23.59296
- second_gains: float32 [512], P(('wide', 'narrow')), may hold values from 32.768 to 131.072
- second_biases: float32 [3584], P(('wide', 'narrow')), may hold values from 65.536 to 262.144
Outputs:
- block_out: bfloat16 [65536, 256], P(('wide', 'narrow'))
- frames_grad: bfloat16 [65536, 256], P(('wide', 'narrow'))
- new_attention: float32 [4, 256, 256], P(None, ('wide', 'narrow'))
- new_in: float32 [256, 2048], P(('wide', 'narrow'))
- new_out: float32 [2048, 256], P(('wide', 'narrow'))
- new_gains: float32 [512], P(('wide', 'narrow'))
- new_biases: float32 [3584], P(('wide', 'narrow'))
- new_first_attention: float32 [4, 256, 256], P(None, ('wide', 'narrow'))
- new_first_in: float32 [256, 2048], P(('wide', 'narrow'))
- new_first_out: float32 [2048, 256], P(('wide', 'narrow'))
- new_first_gains: float32 [512], P(('wide', 'narrow'))
- new_first_biases: float32 [3584], P(('wide', 'narrow'))
- new_second_attention: float32 [4, 256, 256], P(None, ('wide', 'narrow'))
- new_second_in: float32 [256, 2048], P(('wide', 'narrow'))
- new_second_out: float32 [2048, 256], P(('wide', 'narrow'))
- new_second_gains: float32 [512], P(('wide', 'narrow'))
- new_second_biases: float32 [3584], P(('wide', 'narrow'))
The draws below stay inside these ranges and needn't reach their ends.
Inputs may be any that keep to these rules, and one draw needn't show every extreme that they name: `segments`: in each row (one micro-batch of one device) segment numbers never fall and each segment covers 1 to 256 consecutive frames, one exactly 256.
All inputs are finite; a program needn't handle non-finite values.
Results may differ from the reference program's by a relative error of at most 0.0085.
The reference program's roundings to bfloat16 on the way count: a program that leaves them out, or rounds other values in their place, can miss the bound.
Values may be sent and summed in bfloat16 or wider, within the bound.
A program may use at most 128 MiB of HBM per device.

```python
import math
import jax
import jax.numpy as jnp
import numpy as np
from jax import lax

D = 256
HEADS = 4
HD = 64
FF = 2048
BLK = 512
SEGS = 4
STEP = 10
SEG_MOST = 256
BLOCKS = 128
TOKENS = 65536
NBIAS = 3584


def draw_attention_weights(key, part):
    base = jnp.clip(jax.random.normal(key, (4, D, D), jnp.float32), -6.0, 6.0)
    factor = jnp.array([1.3, 1.3, 1.6, 1.6], jnp.float32)
    return base * factor[:, None, None] * D ** (-0.5)


def shard_levels(rng, extent, split, low, high):
    def one(axis_at, shards_of):
        steps = jax.random.uniform(jax.random.fold_in(jax.random.fold_in(rng, 6), axis_at), (shards_of,), jnp.float32, low / len(split), high / len(split))
        return jnp.repeat(jnp.exp(steps), extent[axis_at] // shards_of).reshape((-1,) + (1,) * (len(extent) - axis_at - 1))

    factor_of = one(*split[0])
    for cut in split[1:]:
        factor_of = factor_of * one(*cut)
    return factor_of


def split_up(amount, total, limit, skew):
    weights = [(1 << 20) // math.isqrt(rank ** skew) + 1 for rank in range(2, amount + 1)]
    surplus, given = total - limit - (amount - 1), [1] * (amount - 1)
    while surplus > 0:
        candidates = [i for i in range(amount - 1) if given[i] < limit]
        mass, remaining = sum([weights[i] for i in candidates]), surplus
        for i in candidates:
            addition = min(limit - given[i], max(1, remaining * weights[i] // mass), surplus)
            given[i] = given[i] + addition
            surplus = surplus - addition
    return np.array([limit] + given)


def ragged(key, amount, total, most, slope):
    if amount == 2:
        one = jax.random.randint(key, (), max(1, total - most), min(most, total - 1) + 1)
        return jnp.stack([one, total - one])
    tallies = jnp.asarray(split_up(amount, total, most, slope), jnp.int32)
    twos = (amount - 1) // 2
    donor, sink = tallies[1:1 + 2 * twos:2], tallies[2:2 + 2 * twos:2]
    margin = jnp.minimum(donor - 1, most - sink)
    passed = jax.random.randint(jax.random.fold_in(key, 1), (twos,), 0, 1 << 20) % (margin + 1)
    tallies = tallies.at[1:1 + 2 * twos:2].set(donor - passed).at[2:2 + 2 * twos:2].set(sink + passed)
    return tallies[jax.random.permutation(jax.random.fold_in(key, 2), amount)]


def gaussian(stream_key, dims, spread, bound, split=(), dtype=jnp.bfloat16):
    values = jax.random.normal(stream_key, dims, jnp.float32) * spread
    if len(split) > 0:
        values = shard_levels(stream_key, dims, split, -0.22, 0.18) * values
    return jnp.clip(values, min=-bound, max=bound).astype(dtype)


def setup_inputs(seed: int = 0) -> dict:
    key_of = jax.random.split(jax.random.key(seed), 19)
    frames = gaussian(key_of[0], (TOKENS, D), 1.0, 6.0, ((0, 32),))
    segments = jax.vmap(lambda own: jnp.searchsorted(jnp.cumsum(ragged(own, SEGS, BLK, SEG_MOST, 1)), jnp.arange(BLK), side="right"))(jax.random.split(key_of[1], BLOCKS)).reshape((BLOCKS, BLK)).astype(jnp.int32)
    out_grad = gaussian(key_of[2], (TOKENS, D), 1.0, 6.0, ((0, 32),))
    attention_weights = draw_attention_weights(jax.random.fold_in(key_of[18], 71), 0)
    weight_in = gaussian(key_of[4], (D, FF), D ** -0.5, 0.375, ((0, 32),), jnp.float32)
    weight_out = gaussian(key_of[5], (FF, D), FF ** -0.5, 0.125, ((0, 32),), jnp.float32)
    norm_gains = jnp.clip(1.0 + 0.1 * jax.random.normal(key_of[6], (2 * D,), jnp.float32), 0.5, 1.5)
    biases = gaussian(key_of[7], (NBIAS,), 0.2, 1.2, ((0, 32),), jnp.float32)
    first_attention = gaussian(key_of[8], (4, D, D), (0.033 * TOKENS ** 0.5), 51.2, ((1, 32),), jnp.float32)
    first_in = gaussian(key_of[9], (D, FF), (0.033 * TOKENS ** 0.5), 51.2, ((0, 32),), jnp.float32)
    first_out = gaussian(key_of[10], (FF, D), (0.033 * TOKENS ** 0.5), 51.2, ((0, 32),), jnp.float32)
    first_gains = gaussian(key_of[11], (2 * D,), (0.077 * TOKENS ** 0.5), 115.2, ((0, 32),), jnp.float32)
    first_biases = gaussian(key_of[12], (NBIAS,), (0.077 * TOKENS ** 0.5), 115.2, ((0, 32),), jnp.float32)
    second_attention = jnp.clip(jnp.exp(math.log(23.59296) - 1.3862944 * jax.random.uniform(key_of[13], (4, D, D), jnp.float32) ** shard_levels(key_of[13], (4, D, D), ((1, 32),), -0.2, 0.2)), 5.89824, 23.59296)
    second_in = jnp.clip(jnp.exp(math.log(23.59296) - 1.3862944 * jax.random.uniform(key_of[14], (D, FF), jnp.float32) ** shard_levels(key_of[14], (D, FF), ((0, 32),), -0.2, 0.2)), 5.89824, 23.59296)
    second_out = jnp.clip(jnp.exp(math.log(23.59296) - 1.3862944 * jax.random.uniform(key_of[15], (FF, D), jnp.float32) ** shard_levels(key_of[15], (FF, D), ((0, 32),), -0.2, 0.2)), 5.89824, 23.59296)
    second_gains = jnp.clip(jnp.exp(math.log(131.072) - 1.3862944 * jax.random.uniform(key_of[16], (2 * D,), jnp.float32) ** shard_levels(key_of[16], (2 * D,), ((0, 32),), -0.2, 0.2)), 32.768, 131.072)
    second_biases = jnp.clip(jnp.exp(math.log(262.144) - 1.3862944 * jax.random.uniform(key_of[17], (NBIAS,), jnp.float32) ** shard_levels(key_of[17], (NBIAS,), ((0, 32),), -0.2, 0.2)), 65.536, 262.144)
    return dict(frames=frames, segments=segments, out_grad=out_grad, attention_weights=attention_weights, weight_in=weight_in, weight_out=weight_out, norm_gains=norm_gains, biases=biases, first_attention=first_attention, first_in=first_in, first_out=first_out, first_gains=first_gains, first_biases=first_biases, second_attention=second_attention, second_in=second_in, second_out=second_out, second_gains=second_gains, second_biases=second_biases)


@jax.custom_vjp
def low(v):
    return lax.optimization_barrier(v.astype(jnp.bfloat16)).astype(jnp.float32)

@jax.custom_vjp
def low_back(v):
    return v

def low_keep(v):
    return (low(v), None)

def low_pass(kept, grad):
    return (grad,)

def back_keep(v):
    return (v, None)

def back_low(kept, grad):
    return (low(grad),)
low.defvjp(low_keep, low_pass)
low_back.defvjp(back_keep, back_low)
NORM_EPS = 1e-05
BETA_ONE = 0.9
BETA_TWO = 0.999
ADAM_EPS = 1e-08
RATE_MATRIX = 0.08
RATE_VECTOR = 0.6
WEIGHT_DECAY = 0.01
HIGHEST = lax.Precision.HIGHEST

def layer_norm(values, scale_vec, shift_vec):
    center = values - lax.optimization_barrier(jnp.mean(values, axis=-1, keepdims=True))
    variance = lax.optimization_barrier(jnp.mean(center * center, axis=-1, keepdims=True))
    return center * lax.rsqrt(variance + NORM_EPS) * scale_vec + shift_vec

def block_forward(frame_rows, seg_row, attention_p, inner_p, outer_p, gains_p, biases_p):
    norm_one = low(layer_norm(frame_rows, gains_p[:D], biases_p[4 * D:5 * D]))
    queries = low(low_back(jnp.dot(norm_one, attention_p[0], precision=HIGHEST) + biases_p[:D]))
    keys_mat = low(low_back(jnp.dot(norm_one, attention_p[1], precision=HIGHEST)))
    values = low(low_back(jnp.dot(norm_one, attention_p[2], precision=HIGHEST) + biases_p[D:2 * D]))
    query_heads = queries.reshape(BLK, HEADS, HD)
    key_heads = keys_mat.reshape(BLK, HEADS, HD)
    value_heads = values.reshape(BLK, HEADS, HD)
    scores = low_back(jnp.einsum('qhd,khd->hqk', query_heads, key_heads, precision=HIGHEST) * HD ** (-0.5))
    same_segment = seg_row[:, None] == seg_row[None, :]
    masked = jnp.where(same_segment[None], scores, -1e+30)
    weights_soft = low(jax.nn.softmax(masked, axis=-1))
    mixed_heads = jnp.einsum('hqk,khd->qhd', weights_soft, value_heads, precision=HIGHEST).reshape(BLK, D)
    mixed_heads = low(low_back(mixed_heads))
    middle = frame_rows + low_back(jnp.dot(mixed_heads, attention_p[3], precision=HIGHEST)) + biases_p[2 * D:3 * D]
    norm_two = low(layer_norm(middle, gains_p[D:], biases_p[5 * D:6 * D]))
    hidden = low_back(jnp.dot(norm_two, inner_p, precision=HIGHEST) + biases_p[6 * D:])
    active = low(jax.nn.gelu(hidden))
    return middle + jnp.dot(active, outer_p, precision=HIGHEST) + biases_p[3 * D:4 * D]

def adamw(weight, grad, first, second, rate, decay):
    first_new = BETA_ONE * first + (1.0 - BETA_ONE) * grad
    second_new = BETA_TWO * second + (1.0 - BETA_TWO) * grad * grad
    first_hat = first_new / (1.0 - BETA_ONE ** STEP)
    second_hat = second_new / (1.0 - BETA_TWO ** STEP)
    weight_new = weight - rate * (first_hat / (jnp.sqrt(second_hat) + ADAM_EPS) + decay * weight)
    return (weight_new, first_new, second_new)

def reference(frames, segments, out_grad, attention_weights, weight_in, weight_out, norm_gains, biases, first_attention, first_in, first_out, first_gains, first_biases, second_attention, second_in, second_out, second_gains, second_biases):

    def forward(frame_all, attention_f, inner_f, outer_f, gains_f, biases_f):
        attention_p = low(attention_f)
        inner_p = low(inner_f)
        outer_p = low(outer_f)
        gains_p = low(gains_f)
        biases_p = low(biases_f)

        def one_block(pair):
            return block_forward(pair[0], pair[1], attention_p, inner_p, outer_p, gains_p, biases_p)
        step_fn = jax.checkpoint(one_block)
        blocks = frame_all.reshape(-1, BLK, D)
        return lax.map(step_fn, (blocks, segments)).reshape(-1, D)
    result, pull_back = jax.vjp(forward, frames.astype(jnp.float32), attention_weights, weight_in, weight_out, norm_gains, biases)
    grads = pull_back(out_grad.astype(jnp.float32))
    masters = (attention_weights, weight_in, weight_out, norm_gains, biases)
    firsts = (first_attention, first_in, first_out, first_gains, first_biases)
    seconds = (second_attention, second_in, second_out, second_gains, second_biases)
    rates = (RATE_MATRIX, RATE_MATRIX, RATE_MATRIX, RATE_VECTOR, RATE_VECTOR)
    decays = (WEIGHT_DECAY, WEIGHT_DECAY, WEIGHT_DECAY, 0.0, 0.0)
    updated = [adamw(masters[member], grads[member + 1], firsts[member], seconds[member], rates[member], decays[member]) for member in range(5)]
    return (result.astype(jnp.bfloat16), grads[0].astype(jnp.bfloat16), updated[0][0], updated[1][0], updated[2][0], updated[3][0], updated[4][0], updated[0][1], updated[1][1], updated[2][1], updated[3][1], updated[4][1], updated[0][2], updated[1][2], updated[2][2], updated[3][2], updated[4][2])
```

```python
import functools
import jax
import jax.numpy as jnp
from jax import lax
from jax.experimental import pallas as pl
from jax.experimental.pallas import tpu as pltpu
from jax.sharding import PartitionSpec as P

D = 256
HEADS = 4
HD = 64
FF = 2048
NORM_EPS = 1e-05
C_ONE = 0.7978845608028654
C_THREE = C_ONE * 0.044715
F32 = jnp.float32
BF16 = jnp.bfloat16


MESH = pl.DeviceIdType.MESH


def dot_n(a, b):
    return jnp.dot(a, b, preferred_element_type=F32)


def dot_t(a, b):
    return lax.dot_general(a, b, (((1,), (1,)), ((), ())), preferred_element_type=F32)


def iota(shape, dim):
    return lax.broadcasted_iota(jnp.int32, shape, dim)


def one_hot(cond):
    return jnp.where(cond, 1.0, 0.0).astype(BF16)


def eye():
    return one_hot(iota((D, D), 0) == iota((D, D), 1))


def wide_of(col, width):
    return jnp.concatenate([col] * (width // 128), axis=1)


def lane_fold(v):
    total = v[:, 0:128]
    for at in range(128, v.shape[1], 128):
        total = total + v[:, at : at + 128]
    return total


def col_mean(v):
    return jnp.sum(v, axis=0, keepdims=True) * (1.0 / v.shape[0])


def start_of(seg):
    start = jnp.full((1, 1), 4096.0, F32)
    for v in range(4):
        count = jnp.sum(jnp.where(seg == v, 1.0, 0.0), axis=1, keepdims=True)
        below = jnp.sum(jnp.where(seg < v, 1.0, 0.0), axis=1, keepdims=True)
        start = jnp.minimum(start, jnp.where(count == 256.0, below, 4096.0))
    return start.astype(jnp.int32)


def gelu_both(h):
    h2 = h * h
    t = jnp.tanh(h * (C_THREE * h2 + C_ONE))
    s = 0.5 * t + 0.5
    z = h * s
    slope = s + z * (1.0 - s) * (6.0 * C_THREE * h2 + 2.0 * C_ONE)
    return z, slope


OG1, OG2, OBQ, OBV, OBO, OB2, OC1, OC2, OB1 = 0, 256, 512, 768, 1024, 1280, 1536, 1792, 2048
NVEC = 4096
AG1, AG2, ABQ, ABV, ABO, AB2, AC1, AC2 = range(8)


def scratch_shapes(mb, blk):
    half = blk // 2
    return dict(
        wqkvt=pltpu.VMEM((3 * D, D), BF16),
        wcat=pltpu.VMEM((D, 3 * D), BF16),
        wo=pltpu.VMEM((D, D), BF16),
        wot=pltpu.VMEM((D, D), BF16),
        w1=pltpu.VMEM((D, FF), BF16),
        w1t=pltpu.VMEM((FF, D), BF16),
        w2=pltpu.VMEM((FF, D), BF16),
        w2t=pltpu.VMEM((D, FF), BF16),
        col=pltpu.VMEM((NVEC, 128), F32),
        vh1=pltpu.VMEM((mb, D, blk), F32),
        rs1=pltpu.VMEM((mb, 8, blk), F32),
        vh2=pltpu.VMEM((mb, D, blk), F32),
        rs2=pltpu.VMEM((mb, 8, blk), F32),
        at=pltpu.VMEM((mb, D, blk), BF16),
        bt=pltpu.VMEM((mb, D + 16, blk), BF16),
        gt=pltpu.VMEM((mb, D, blk), BF16),
        qt=pltpu.VMEM((mb, D, blk), BF16),
        kt=pltpu.VMEM((mb, D, blk), BF16),
        vt=pltpu.VMEM((mb, D, blk), BF16),
        kn=pltpu.VMEM((mb, blk, D), BF16),
        vn=pltpu.VMEM((mb, blk, D), BF16),
        ot=pltpu.VMEM((mb, D, blk), BF16),
        prob=pltpu.VMEM((mb, 2, HEADS, half, half), F32),
        out=pltpu.VMEM((mb, D, blk), F32),
        db=pltpu.VMEM((mb, D, blk), F32),
        hs=pltpu.VMEM((2, 512, blk), F32),
        dz=pltpu.VMEM((2, 512, blk), F32),
        zb=pltpu.VMEM((2, 512, blk), BF16),
        dh=pltpu.VMEM((2, 512, blk), BF16),
        dqkv=pltpu.VMEM((2, 3 * D, blk), BF16),
        acc=pltpu.VMEM((8, D, 128), F32),
        g1=pltpu.VMEM((D + 16, FF), F32),
        g2=pltpu.VMEM((FF, D), F32),
        ga=pltpu.VMEM((D, 4 * D), F32),
    )


def transpose_weights_attention(s):
    unit = eye()
    for c in range(3):
        s.wqkvt[c * D : (c + 1) * D, :] = dot_t(unit, s.wcat[:, c * D : (c + 1) * D]).astype(BF16)
    s.wot[...] = dot_t(unit, s.wo[...]).astype(BF16)


def transpose_weights_inner(s):
    unit = eye()
    for c in range(FF // D):
        cs = slice(c * D, (c + 1) * D)
        s.w1t[cs, :] = dot_t(unit, s.w1[:, cs]).astype(BF16)
        s.w2t[:, cs] = dot_t(unit, s.w2[cs, :]).astype(BF16)


def col_of(s, at, width):
    return wide_of(s.col[at : at + D, :], width)


def load_rows(s, m, x_ref, g_ref, seg_ref, blk):
    start = start_of(seg_ref[m : m + 1, :])
    rows = slice(m * blk, (m + 1) * blk)
    diff = iota((blk, blk), 1) - iota((blk, blk), 0)
    perm = one_hot((diff == start) | (diff == start - blk))
    both = jnp.concatenate([x_ref[rows, :], g_ref[rows, :]], axis=1)
    rolled = dot_n(perm, both).astype(BF16)
    unit = eye()
    xt = dot_t(unit, rolled[:, 0:D])
    gt = dot_t(unit, rolled[:, D : 2 * D])
    s.gt[m] = gt.astype(BF16)
    s.acc[AB2] = lane_fold(gt) if m == 0 else s.acc[AB2] + lane_fold(gt)
    s.out[m] = xt
    center = xt - col_mean(xt)
    rs = lax.rsqrt(col_mean(center * center) + NORM_EPS)
    s.vh1[m] = center * rs
    s.rs1[m] = jnp.broadcast_to(rs, (8, blk))
    seg = seg_ref[m : m + 1, :].astype(F32).astype(BF16)
    tail = perm[blk // 2 :, :]
    seg_row = dot_t(jnp.broadcast_to(seg, (16, blk)), tail)[0:1, :]
    seg_col = dot_t(tail, jnp.broadcast_to(seg, (128, blk)))
    return jnp.where(wide_of(seg_col, blk // 2) == seg_row, 0.0, -1e30)


def project(s, m, blk):
    a = (s.vh1[m] * col_of(s, OG1, blk) + col_of(s, OC1, blk)).astype(BF16)
    s.at[m] = a
    qkv = dot_n(s.wqkvt[...], a)
    q = (qkv[0:D] + col_of(s, OBQ, blk)).astype(BF16)
    s.qt[m] = q * jnp.asarray(HD ** (-0.5), BF16)
    k = qkv[D : 2 * D].astype(BF16)
    v = (qkv[2 * D :] + col_of(s, OBV, blk)).astype(BF16)
    s.kt[m] = k
    s.vt[m] = v
    unit = eye()
    for at in range(0, blk, D):
        s.kn[m, at : at + D, :] = dot_t(unit, k[:, at : at + D]).astype(BF16)
        s.vn[m, at : at + D, :] = dot_t(unit, v[:, at : at + D]).astype(BF16)


def pair_rows(v, head):
    zero = jnp.zeros_like(v)
    return jnp.concatenate([v, zero] if head % 2 == 0 else [zero, v], axis=0)


def attend(s, m, bias, blk):
    half = blk // 2
    for part in range(2):
        qs = slice(part * half, (part + 1) * half)
        for head in range(HEADS):
            hr = slice(head * HD, (head + 1) * HD)
            pc = slice((head // 2) * 128, (head // 2) * 128 + 128)
            st = dot_n(s.kn[m, qs, pc], pair_rows(s.qt[m, hr, qs], head))
            if part == 1:
                st = st + bias
            peak = jnp.max(st, axis=0, keepdims=True)
            e = jnp.exp(st - peak)
            total = jnp.sum(e, axis=0, keepdims=True)
            prob = e * (1.0 / total)
            s.prob[m, part, head] = prob
            s.ot[m, hr, qs] = dot_n(s.vt[m, hr, qs], prob.astype(BF16)).astype(BF16)


def middle(s, m, blk):
    y = s.out[m] + dot_n(s.wot[...], s.ot[m]) + col_of(s, OBO, blk)
    center = y - col_mean(y)
    rs = lax.rsqrt(col_mean(center * center) + NORM_EPS)
    vhat = center * rs
    s.vh2[m] = vhat
    s.rs2[m] = jnp.broadcast_to(rs, (8, blk))
    s.bt[m, 0:D, :] = (vhat * col_of(s, OG2, blk) + col_of(s, OC2, blk)).astype(BF16)
    s.bt[m, D:, :] = jnp.ones((16, blk), BF16)
    s.out[m] = y + col_of(s, OB2, blk)


def feed_forward(s, mb, blk, fc=512, br=32, hook=None):
    steps = [(c, m) for c in range(FF // fc) for m in range(mb)]

    def pre(i):
        c, m = steps[i]
        cs = slice(c * fc, (c + 1) * fc)
        s.hs[i % 2] = dot_n(s.w1t[cs, :], s.bt[m, 0:D, :])
        s.dz[i % 2] = dot_n(s.w2[cs, :], s.gt[m])

    def mid(i):
        c, m = steps[i]
        p = i % 2
        for r in range(0, fc, br):
            rs = slice(r, r + br)
            bias = wide_of(s.col[OB1 + c * fc + r : OB1 + c * fc + r + br, :], blk)
            z, slope = gelu_both(s.hs[p, rs, :] + bias)
            s.zb[p, rs, :] = z.astype(BF16)
            s.dh[p, rs, :] = (s.dz[p, rs, :] * slope).astype(BF16)

    def post(i):
        c, m = steps[i]
        cs = slice(c * fc, (c + 1) * fc)
        p = i % 2
        z, dh = s.zb[p], s.dh[p]
        s.out[m] = s.out[m] + dot_n(s.w2t[:, cs], z)
        d = dot_n(s.w1[:, cs], dh)
        s.db[m] = d if c == 0 else s.db[m] + d
        g2 = dot_t(z, s.gt[m])
        g1 = dot_t(s.bt[m], dh)
        s.g2[cs, :] = g2 if m == 0 else s.g2[cs, :] + g2
        s.g1[:, cs] = g1 if m == 0 else s.g1[:, cs] + g1

    for i in range(-1, len(steps) + 1):
        if i + 1 < len(steps):
            pre(i + 1)
        if 0 <= i < len(steps):
            mid(i)
        if i >= 1:
            post(i - 1)
            if hook is not None and (i - 1) % mb == mb - 1:
                hook((i - 1) // mb)


def norm_back(s, u, vhat, rs, gain_at):
    gu = u * col_of(s, gain_at, u.shape[1])
    return (gu - col_mean(gu) - vhat * col_mean(gu * vhat)) * rs


def add_to(s, which, m, value):
    s.acc[which] = value if m == 0 else s.acc[which] + value


def unroll_rows(s, m, value, seg_ref, ref, blk):
    start = start_of(seg_ref[m : m + 1, :])
    diff = iota((blk, blk), 0) - iota((blk, blk), 1)
    perm = one_hot((diff == start) | (diff == start - blk))
    ref[m * blk : (m + 1) * blk, :] = dot_t(perm, value).astype(BF16)


def back_middle(s, m, seg_ref, out_ref, blk):
    unroll_rows(s, m, s.out[m].astype(BF16), seg_ref, out_ref, blk)
    u = s.db[m]
    vhat = s.vh2[m]
    add_to(s, AG2, m, lane_fold(u * vhat))
    add_to(s, AC2, m, lane_fold(u))
    dy = s.gt[m].astype(F32) + norm_back(s, u, vhat, s.rs2[m, 0:1, :], OG2)
    s.out[m] = dy
    add_to(s, ABO, m, lane_fold(dy))
    dp = dy.astype(BF16)
    gwo = dot_t(s.ot[m], dp)
    s.ga[:, 3 * D :] = gwo if m == 0 else s.ga[:, 3 * D :] + gwo
    s.bt[m, 0:D, :] = dot_n(s.wo[...], dp).astype(BF16)


def back_attend(s, m, blk):
    half = blk // 2
    scale = HD ** (-0.5)
    for part in range(2):
        qs = slice(part * half, (part + 1) * half)
        for head in range(HEADS):
            hr = slice(head * HD, (head + 1) * HD)
            pc = slice((head // 2) * 128, (head // 2) * 128 + 128)
            do = s.bt[m, hr, qs]
            da = dot_n(s.vn[m, qs, pc], pair_rows(do, head))
            prob = s.prob[m, part, head]
            weighted = prob * da
            delta = jnp.sum(weighted, axis=0, keepdims=True)
            ds = (weighted - prob * delta).astype(BF16)
            dv = dot_t(do, prob.astype(BF16))
            dq = dot_n(s.kt[m, hr, qs], ds) * scale
            dk = dot_t(s.qt[m, hr, qs], ds)
            s.dqkv[m % 2, head * HD : head * HD + HD, qs] = dq.astype(BF16)
            s.dqkv[m % 2, D + head * HD : D + head * HD + HD, qs] = dk.astype(BF16)
            s.dqkv[m % 2, 2 * D + head * HD : 2 * D + head * HD + HD, qs] = dv.astype(BF16)


def back_project(s, m, seg_ref, dx_ref, blk):
    dqkv = s.dqkv[m % 2]
    add_to(s, ABQ, m, lane_fold(dqkv[0:D].astype(F32)))
    add_to(s, ABV, m, lane_fold(dqkv[2 * D :].astype(F32)))
    g = dot_t(s.at[m], dqkv)
    s.ga[:, 0 : 3 * D] = g if m == 0 else s.ga[:, 0 : 3 * D] + g
    u = dot_n(s.wcat[...], dqkv)
    vhat = s.vh1[m]
    add_to(s, AG1, m, lane_fold(u * vhat))
    add_to(s, AC1, m, lane_fold(u))
    dx = s.out[m] + norm_back(s, u, vhat, s.rs1[m, 0:1, :], OG1)
    unroll_rows(s, m, dx.astype(BF16), seg_ref, dx_ref, blk)


def vector_row(s):
    ones = jnp.ones((16, 128), BF16)
    rows = []
    for which in range(8):
        v = s.acc[which]
        high = v.astype(BF16)
        low = (v - high.astype(F32)).astype(BF16)
        rows.append((dot_t(ones, high) + dot_t(ones, low))[0:8, :])
    return jnp.concatenate(rows + [s.g1[D : D + 8, :]], axis=1)


class Names:
    def __init__(self, keys, refs):
        for key, ref in zip(keys, refs):
            setattr(self, key, ref)


MSG = 40


class Place:
    def __init__(self):
        wide = lax.axis_index("wide")
        narrow = lax.axis_index("narrow")
        self.z, self.y = lax.div(wide, 2), lax.rem(wide, 2)
        self.x, self.core = lax.div(narrow, 2), lax.rem(narrow, 2)

    def near_z(self, k):
        z = lax.rem(self.z + k, 4)
        return (z * 2 + self.y, self.x * 2 + self.core)

    def flip(self, k):
        x = self.x + (k % 2) * (1 - 2 * self.x)
        y = self.y + (k // 2) * (1 - 2 * self.y)
        return y, x

    def near_plane(self, k):
        y, x = self.flip(k)
        return (self.z * 2 + y, x * 2 + self.core)

    def sibling(self):
        return (self.z * 2 + self.y, self.x * 2 + 1 - self.core)

    def slot(self):
        return self.core * 16 + self.y * 8 + self.x * 4 + self.z

    def group(self, k):
        y, x = self.flip(k)
        return y * 8 + x * 4


def remote(src, dst, send, recv, device):
    return pltpu.make_async_remote_copy(
        src_ref=src, dst_ref=dst, send_sem=send, recv_sem=recv, device_id=device, device_id_type=MESH
    )


def greet(place):
    barrier = pltpu.get_barrier_semaphore()
    partners = [place.near_z(k) for k in (1, 2, 3)]
    partners += [place.near_plane(k) for k in (1, 2, 3)] + [place.sibling()]
    for partner in partners:
        pl.semaphore_signal(barrier, inc=1, device_id=partner, device_id_type=MESH)
    pl.semaphore_wait(barrier, len(partners))


class Gather:
    def __init__(self, place, buf, send, recv):
        own = place.slot()
        self.first = [
            remote(buf.at[own], buf.at[own], send.at[k - 1], recv.at[k - 1], place.near_z(k))
            for k in (1, 2, 3)
        ]
        mine = pl.ds(place.core * 16 + place.group(0), 4)
        self.second = [
            remote(buf.at[mine], buf.at[mine], send.at[2 + k], recv.at[2 + k], place.near_plane(k))
            for k in (1, 2, 3)
        ]
        self.third = []
        for k in range(4):
            at = pl.ds(place.core * 16 + place.group(k), 4)
            self.third.append(
                remote(buf.at[at], buf.at[at], send.at[6 + k], recv.at[6 + k], place.sibling())
            )

    def start_first(self):
        for copy in self.first:
            copy.start()

    def start_second(self):
        for copy in self.first:
            copy.wait_recv()
        for copy in self.second:
            copy.start()
        self.third[0].start()

    def start_third(self):
        for copy, after in zip(self.second, self.third[1:]):
            copy.wait_recv()
            after.start()

    def finish(self):
        for copy in self.third:
            copy.wait_recv()
        for copy in self.first + self.second + self.third:
            copy.wait_send()


class Scatter:
    def __init__(self, place, own, buf, got, held, send, recv):
        self.place, self.own, self.buf, self.got, self.held = place, own, buf, got, held
        self.first = []
        for k in range(4):
            at = pl.ds(place.group(k), 4)
            self.first.append(
                remote(buf.at[at], got.at[at], send.at[k], recv.at[k], place.sibling())
            )
        self.second, self.third = [], []
        for k in (1, 2, 3):
            at = pl.ds(12 + 4 * k, 4)
            self.second.append(
                remote(buf.at[at], got.at[at], send.at[3 + k], recv.at[3 + k], place.near_plane(k))
            )
            self.third.append(
                remote(
                    buf.at[27 + k], got.at[27 + k], send.at[6 + k], recv.at[6 + k], place.near_z(k)
                )
            )

    def start_first(self):
        other = 1 - self.place.core
        for y in range(2):
            for x in range(2):
                for z in range(4):
                    term = self.own(z * 8 + y * 4 + x * 2 + other)
                    self.buf[y * 8 + x * 4 + z] = term.astype(BF16)
        for k in (3, 1, 2, 0):
            self.first[k].start()

    def start_second(self):
        place = self.place
        for k in (3, 1, 2, 0):
            self.first[k].wait_recv()
            y, x = place.flip(k)
            for z in range(4):
                term = self.own(z * 8 + y * 4 + x * 2 + place.core)
                term = term + self.got[place.group(k) + z].astype(F32)
                if k == 0:
                    self.held[z] = term
                else:
                    self.buf[12 + 4 * k + z] = term.astype(BF16)
            if k > 0:
                self.second[k - 1].start()

    def start_third(self):
        for copy in self.second:
            copy.wait_recv()
        for z in range(4):
            term = self.held[z]
            for k in (1, 2, 3):
                term = term + self.got[12 + 4 * k + z].astype(F32)
            self.held[z] = term
        for k in (1, 2, 3):
            self.buf[27 + k] = self.held[lax.rem(self.place.z + k, 4)].astype(BF16)
            self.third[k - 1].start()

    def finish(self):
        term = self.held[self.place.z]
        for k in (1, 2, 3):
            self.third[k - 1].wait_recv()
            term = term + self.got[27 + k].astype(F32)
        for copy in self.first + self.second + self.third:
            copy.wait_send()
        return term


def slot_of(device):
    return (device % 2) * 16 + (device // 4 % 2) * 8 + (device // 2 % 2) * 4 + device // 8


def entry_place(shape, dim):
    k = iota(shape, dim).astype(F32)
    rest = k - 512.0
    gain = k < 512.0
    device = jnp.where(gain, jnp.floor((k + 0.5) * (1.0 / 16)), jnp.floor((rest + 0.5) * (1.0 / 112)))
    lane = jnp.where(gain, k - 16.0 * device, rest - 112.0 * device + 16.0)
    return device, lane


def slot_number(device):
    z = jnp.floor((device + 0.5) * 0.125)
    rest = device - 8.0 * z
    y = jnp.floor((rest + 0.5) * 0.25)
    rest = rest - 4.0 * y
    x = jnp.floor((rest + 0.5) * 0.5)
    core = rest - 2.0 * x
    return core * 16.0 + y * 8.0 + x * 4.0 + z


def unpack_attention(s):
    for c in range(4):
        rows = [s.bufa[slot_of(d), 8 * c : 8 * c + 8, :].astype(F32) for d in range(32)]
        full = jnp.concatenate(rows, axis=0).astype(BF16)
        if c < 3:
            s.wcat[:, c * D : (c + 1) * D] = full
        else:
            s.wo[...] = full
    rows = [s.bufa[d, 32:40, 0:128].astype(F32) for d in range(32)]
    table = jnp.concatenate(rows, axis=0).astype(BF16)
    ones = jnp.ones((128, 128), BF16)
    step = 512
    for at in range(0, NVEC, step):
        k = (iota((step, 256), 0) + at).astype(F32)
        gain = k < 512.0
        rest = k - 512.0
        device = jnp.where(
            gain, jnp.floor((k + 0.5) * (1.0 / 16)), jnp.floor((rest + 0.5) * (1.0 / 112))
        )
        lane = jnp.where(gain, k - 16.0 * device, rest - 112.0 * device + 16.0)
        pick = one_hot(slot_number(device) * 8.0 == iota((step, 256), 1).astype(F32))
        found = dot_n(pick, table)
        keep = lane[:, 0:128] == iota((step, 128), 1).astype(F32)
        s.col[at : at + step, :] = dot_n(jnp.where(keep, found, 0.0).astype(BF16), ones)


def unpack_inner(s):
    for i in range(16):
        pair = [s.buf1[slot_of(2 * i + c)].astype(F32) for c in range(2)]
        s.w1[16 * i : 16 * i + 16, :] = jnp.concatenate(pair, axis=0).astype(BF16)
    for d in range(32):
        s.w2[64 * d : 64 * d + 64, :] = s.buf2[slot_of(d)]


def vector_rows(s):
    row = vector_row(s)[0:1, :]
    high = row.astype(BF16).astype(F32)
    device, _ = entry_place((32, NVEC), 1)
    mine = device == iota((32, NVEC), 0).astype(F32)
    total = None
    k = iota((NVEC, 128), 0).astype(F32)
    rest = k - 512.0
    device = jnp.where(
        k < 512.0, jnp.floor((k + 0.5) * (1.0 / 16)), jnp.floor((rest + 0.5) * (1.0 / 112))
    )
    lane = jnp.where(k < 512.0, k - 16.0 * device, rest - 112.0 * device + 16.0)
    pick = one_hot(lane == iota((NVEC, 128), 1).astype(F32))
    for term in (high, row - high):
        part = dot_n(jnp.where(mine, term, 0.0).astype(BF16), pick)
        total = part if total is None else total + part
    high = total.astype(BF16).astype(F32)
    s.vrow[:, 0:128] = high
    s.vrow[:, 128:256] = total - high


def own_attention(s):
    def load(device):
        rows = pl.ds(pl.multiple_of(device * 8, 8), 8)
        parts = [s.ga[rows, c * D : (c + 1) * D] for c in range(4)]
        vector = jnp.broadcast_to(s.vrow[pl.ds(device, 1), :], (8, D))
        return jnp.concatenate(parts + [vector], axis=0)

    return load


def own_first(s):
    return lambda device: s.g1[pl.ds(pl.multiple_of(device * 8, 8), 8), :]


def own_second(s):
    return lambda device: s.g2[pl.ds(pl.multiple_of(device * 64, 64), 64), :]


def fused_scratch(mb, blk):
    shapes = scratch_shapes(mb, blk)
    for name, (rows, cols) in (("a", (MSG, D)), ("1", (8, FF)), ("2", (64, D))):
        shapes["buf" + name] = pltpu.VMEM((32, rows, cols), BF16)
        shapes["got" + name] = pltpu.VMEM((31, rows, cols), BF16)
        shapes["held" + name] = pltpu.VMEM((4, rows, cols), F32)
        shapes["gsend" + name] = pltpu.SemaphoreType.DMA((10,))
        shapes["grecv" + name] = pltpu.SemaphoreType.DMA((10,))
        shapes["ssend" + name] = pltpu.SemaphoreType.DMA((10,))
        shapes["srecv" + name] = pltpu.SemaphoreType.DMA((10,))
    shapes["vrow"] = pltpu.VMEM((32, D), F32)
    shapes["line"] = pltpu.VMEM((8, D), F32)
    return shapes


def fused_kernel(keys, mb, blk, *refs):
    x_ref, seg_ref, g_ref, wa, w1, w2, gains, biases = refs[:8]
    out_ref, dx_ref, suma, sum1, sum2 = refs[8:13]
    s = Names(keys, refs[13:])
    place = Place()
    own = place.slot()
    s.line[...] = jnp.zeros((8, D), F32)
    s.line[0:1, 0:16] = gains[...]
    s.line[0:1, 16:128] = biases[...]
    s.bufa[own] = jnp.concatenate([wa[c] for c in range(4)] + [s.line[...]], axis=0).astype(BF16)
    s.buf1[own] = w1[...].astype(BF16)
    s.buf2[own] = w2[...].astype(BF16)
    greet(place)
    gather = [
        Gather(place, getattr(s, "buf" + n), getattr(s, "gsend" + n), getattr(s, "grecv" + n))
        for n in "a12"
    ]
    for g in gather:
        g.start_first()
    bias = [load_rows(s, 0, x_ref, g_ref, seg_ref, blk)]
    gather[0].start_second()
    bias.append(load_rows(s, 1, x_ref, g_ref, seg_ref, blk))
    gather[0].start_third()
    for m in range(2, mb):
        bias.append(load_rows(s, m, x_ref, g_ref, seg_ref, blk))
    gather[0].finish()
    for g in gather[1:]:
        g.start_second()
    unpack_attention(s)
    transpose_weights_attention(s)
    for m in range(mb):
        project(s, m, blk)
        attend(s, m, bias[m], blk)
        middle(s, m, blk)
        if m == 1:
            for g in gather[1:]:
                g.start_third()
    for g in gather[1:]:
        g.finish()
    unpack_inner(s)
    transpose_weights_inner(s)
    feed_forward(s, mb, blk)
    scatter = [
        Scatter(
            place,
            load(s),
            getattr(s, "buf" + n),
            getattr(s, "got" + n),
            getattr(s, "held" + n),
            getattr(s, "ssend" + n),
            getattr(s, "srecv" + n),
        )
        for n, load in (("a", own_attention), ("1", own_first), ("2", own_second))
    ]
    for t in scatter[1:]:
        t.start_first()
    for m in range(mb):
        back_middle(s, m, seg_ref, out_ref, blk)
        back_attend(s, m, blk)
        back_project(s, m, seg_ref, dx_ref, blk)
        if m == 0:
            for t in scatter[1:]:
                t.start_second()
        if m == 2:
            for t in scatter[1:]:
                t.start_third()
    vector_rows(s)
    scatter[0].start_first()
    scatter[0].start_second()
    sum1[...] = scatter[1].finish()
    sum2[...] = scatter[2].finish()
    scatter[0].start_third()
    suma[...] = scatter[0].finish()


STEP = 10
BETA_ONE = 0.9
BETA_TWO = 0.999
ADAM_EPS = 1e-08
RATES = (0.08, 0.08, 0.08, 0.6, 0.6)
DECAYS = (0.01, 0.01, 0.01, 0.0, 0.0)


def adamw(weight, grad, first, second, rate, decay):
    first_new = BETA_ONE * first + (1.0 - BETA_ONE) * grad
    second_new = BETA_TWO * second + (1.0 - BETA_TWO) * grad * grad
    first_hat = first_new / (1.0 - BETA_ONE**STEP)
    second_hat = second_new / (1.0 - BETA_TWO**STEP)
    weight_new = weight - rate * (first_hat / (jnp.sqrt(second_hat) + ADAM_EPS) + decay * weight)
    return weight_new, first_new, second_new


def adam_kernel(*refs):
    suma, sum1, sum2 = refs[:3]
    state, new = refs[3:18], refs[18:]

    def update(member, grad, at=()):
        at = at if at else (slice(None),)
        values = adamw(
            state[member][at], grad, state[5 + member][at], state[10 + member][at], RATES[member], DECAYS[member]
        )
        for kind in range(3):
            new[5 * kind + member][at] = values[kind]

    for c in range(4):
        update(0, suma[8 * c : 8 * c + 8, :], (c,))
    update(1, sum1[...])
    update(2, sum2[...])
    line = suma[32:33, 0:128] + suma[32:33, 128:256]
    update(3, line[:, 0:16])
    update(4, line[:, 16:128])


VMEM_SPEC = pl.BlockSpec(memory_space=pltpu.VMEM)


def fused_device(*args):
    frames, segments, out_grad = args[:3]
    rows = lambda v: v.reshape(1, -1) if v.ndim == 1 else v
    state = [rows(v) for v in args[3:]]
    mb, blk = segments.shape
    shapes = fused_scratch(mb, blk)
    like = lambda v: jax.ShapeDtypeStruct(v.shape, v.dtype)
    out, dx, suma, sum1, sum2 = pl.pallas_call(
        functools.partial(fused_kernel, list(shapes), mb, blk),
        out_shape=[like(frames), like(frames)]
        + [jax.ShapeDtypeStruct(t, F32) for t in ((MSG, D), (8, FF), (64, D))],
        in_specs=[VMEM_SPEC] * 8,
        out_specs=[VMEM_SPEC] * 5,
        scratch_shapes=list(shapes.values()),
        compiler_params=pltpu.CompilerParams(
            collective_id=0, has_side_effects=True, vmem_limit_bytes=63 * 2**20
        ),
    )(frames, segments, out_grad, *state[:5])
    new = pl.pallas_call(
        adam_kernel,
        out_shape=[like(v) for v in state],
        in_specs=[VMEM_SPEC] * 18,
        out_specs=[VMEM_SPEC] * 15,
    )(suma, sum1, sum2, *state)
    return (out, dx, *[v.reshape(t.shape) for v, t in zip(new, args[3:])])


def local_kernel(keys, mb, blk, *refs):
    x_ref, seg_ref, g_ref, wa, w1, w2, col = refs[:7]
    out_ref, dx_ref, ga, g1, g2, gv = refs[7:13]
    s = Names(keys, refs[13:])
    for c in range(3):
        s.wcat[:, c * D : (c + 1) * D] = wa[c]
    s.wo[...] = wa[3]
    s.w1[...] = w1[...]
    s.w2[...] = w2[...]
    s.col[...] = col[...]
    transpose_weights_attention(s)
    transpose_weights_inner(s)
    for m in range(mb):
        bias = load_rows(s, m, x_ref, g_ref, seg_ref, blk)
        project(s, m, blk)
        attend(s, m, bias, blk)
        middle(s, m, blk)
    feed_forward(s, mb, blk)
    for m in range(mb):
        back_middle(s, m, seg_ref, out_ref, blk)
        back_attend(s, m, blk)
        back_project(s, m, seg_ref, dx_ref, blk)
    gv[...] = vector_row(s)
    ga[...] = s.ga[...]
    g1[...] = s.g1[0:D, :]
    g2[...] = s.g2[...]


AXES = ("wide", "narrow")


def local_device(*args):
    frames, segments, out_grad = args[:3]
    weights, firsts, seconds = args[3:8], args[8:13], args[13:18]
    dims = (1, 0, 0, 0, 0)
    full = [
        lax.all_gather(w.astype(BF16), AXES, axis=dim, tiled=True) for w, dim in zip(weights, dims)
    ]
    mb, blk = segments.shape
    table = jnp.concatenate([full[3], full[4]]).astype(F32)
    shapes = scratch_shapes(mb, blk)
    like = lambda v: jax.ShapeDtypeStruct(v.shape, v.dtype)
    out, dx, ga, g1, g2, gv = pl.pallas_call(
        functools.partial(local_kernel, list(shapes), mb, blk),
        out_shape=[like(frames), like(frames)]
        + [jax.ShapeDtypeStruct(t, F32) for t in ((D, 4 * D), (D, FF), (FF, D), (8, NVEC))],
        in_specs=[VMEM_SPEC] * 7,
        out_specs=[VMEM_SPEC] * 6,
        scratch_shapes=list(shapes.values()),
        compiler_params=pltpu.CompilerParams(vmem_limit_bytes=63 * 2**20),
    )(frames, segments, out_grad, *full[:3], jnp.broadcast_to(table[:, None], (NVEC, 128)))
    grads = (jnp.stack(jnp.split(ga, 4, axis=1)), g1, g2, gv[0, :512], gv[0, 512:])
    owned = [
        lax.psum_scatter(g, AXES, scatter_dimension=dim, tiled=True) for g, dim in zip(grads, dims)
    ]
    new = [adamw(*v) for v in zip(weights, owned, firsts, seconds, RATES, DECAYS)]
    return (out, dx, *[new[member][kind] for kind in range(3) for member in range(5)])


def solution(mesh):
    rows, matrix, vector = P(AXES, None), P(None, AXES, None), P(AXES)
    group = (matrix, rows, rows, vector, vector)
    fits = (mesh.shape["wide"], mesh.shape["narrow"]) == (8, 4)
    return jax.shard_map(
        fused_device if fits else local_device,
        mesh=mesh,
        in_specs=(rows, rows, rows, *group, *group, *group),
        out_specs=(rows, rows, *group, *group, *group),
        check_vma=False,
    )
```

```python
import functools
import jax
import jax.numpy as jnp
from jax import lax
from jax.experimental import pallas as pl
from jax.experimental.pallas import tpu as pltpu
from jax.sharding import PartitionSpec as P

D = 256
HEADS = 4
HD = 64
FF = 2048
NORM_EPS = 1e-05
C_ONE = 0.7978845608028654
C_THREE = C_ONE * 0.044715
F32 = jnp.float32
BF16 = jnp.bfloat16


MESH = pl.DeviceIdType.MESH


def dot_n(a, b):
    return jnp.dot(a, b, preferred_element_type=F32)


def dot_t(a, b):
    return lax.dot_general(a, b, (((1,), (1,)), ((), ())), preferred_element_type=F32)


def iota(shape, dim):
    return lax.broadcasted_iota(jnp.int32, shape, dim)


def one_hot(cond):
    return jnp.where(cond, 1.0, 0.0).astype(BF16)


def eye():
    return one_hot(iota((D, D), 0) == iota((D, D), 1))


def wide_of(col, width):
    return jnp.concatenate([col] * (width // 128), axis=1)


def lane_fold(v):
    total = v[:, 0:128]
    for at in range(128, v.shape[1], 128):
        total = total + v[:, at : at + 128]
    return total


def col_mean(v):
    return jnp.sum(v, axis=0, keepdims=True) * (1.0 / v.shape[0])


def start_of(seg):
    start = jnp.full((1, 1), 4096.0, F32)
    for v in range(4):
        count = jnp.sum(jnp.where(seg == v, 1.0, 0.0), axis=1, keepdims=True)
        below = jnp.sum(jnp.where(seg < v, 1.0, 0.0), axis=1, keepdims=True)
        start = jnp.minimum(start, jnp.where(count == 256.0, below, 4096.0))
    return start.astype(jnp.int32)


def gelu_both(h):
    h2 = h * h
    t = jnp.tanh(h * (C_THREE * h2 + C_ONE))
    s = 0.5 * t + 0.5
    z = h * s
    slope = s + z * (1.0 - s) * (6.0 * C_THREE * h2 + 2.0 * C_ONE)
    return z, slope


OG1, OG2, OBQ, OBV, OBO, OB2, OC1, OC2, OB1 = 0, 256, 512, 768, 1024, 1280, 1536, 1792, 2048
NVEC = 4096
AG1, AG2, ABQ, ABV, ABO, AB2, AC1, AC2 = range(8)


def scratch_shapes(mb, blk):
    half = blk // 2
    return dict(
        wqkvt=pltpu.VMEM((3 * D, D), BF16),
        wcat=pltpu.VMEM((D, 3 * D), BF16),
        wo=pltpu.VMEM((D, D), BF16),
        wot=pltpu.VMEM((D, D), BF16),
        w1=pltpu.VMEM((D, FF), BF16),
        w1t=pltpu.VMEM((FF, D), BF16),
        w2=pltpu.VMEM((FF, D), BF16),
        w2t=pltpu.VMEM((D, FF), BF16),
        col=pltpu.VMEM((NVEC, 128), BF16),
        vh1=pltpu.VMEM((mb, D, blk), F32),
        rs1=pltpu.VMEM((mb, 8, blk), F32),
        bias=pltpu.VMEM((mb, half, half), BF16),
        vh2=pltpu.VMEM((mb, D, blk), F32),
        rs2=pltpu.VMEM((mb, 8, blk), F32),
        at=pltpu.VMEM((mb, D, blk), BF16),
        bt=pltpu.VMEM((mb, D + 16, blk), BF16),
        gt=pltpu.VMEM((mb, D, blk), BF16),
        qt=pltpu.VMEM((mb, D, blk), BF16),
        kt=pltpu.VMEM((mb, D, blk), BF16),
        vt=pltpu.VMEM((mb, D, blk), BF16),
        vn=pltpu.VMEM((mb, blk, D), BF16),
        ot=pltpu.VMEM((mb, D, blk), BF16),
        prob=pltpu.VMEM((mb, 2, HEADS, half, half), BF16),
        out=pltpu.VMEM((mb, D, blk), F32),
        db=pltpu.VMEM((mb, D, blk), F32),
        hs=pltpu.VMEM((2, 512, blk), F32),
        dz=pltpu.VMEM((2, 512, blk), F32),
        zb=pltpu.VMEM((2, 512, blk), BF16),
        dh=pltpu.VMEM((2, 512, blk), BF16),
        dqkv=pltpu.VMEM((2, 3 * D, blk), BF16),
        acc=pltpu.VMEM((8, D, 128), F32),
        g1=pltpu.VMEM((D + 16, FF), F32),
        g2=pltpu.VMEM((FF, D), F32),
        ga=pltpu.VMEM((D, 4 * D), F32),
    )


def transpose_weights_attention(s):
    unit = eye()
    for c in range(3):
        s.wqkvt[c * D : (c + 1) * D, :] = dot_t(unit, s.wcat[:, c * D : (c + 1) * D]).astype(BF16)
    s.wot[...] = dot_t(unit, s.wo[...]).astype(BF16)


def transpose_weights_inner(s):
    unit = eye()
    for c in range(FF // D):
        cs = slice(c * D, (c + 1) * D)
        s.w1t[cs, :] = dot_t(unit, s.w1[:, cs]).astype(BF16)
        s.w2t[:, cs] = dot_t(unit, s.w2[cs, :]).astype(BF16)


def col_of(s, at, width):
    return wide_of(s.col[at : at + D, :].astype(F32), width)


def norm_of(v):
    center = v - col_mean(v)
    rs = lax.rsqrt(col_mean(center * center) + NORM_EPS)
    return center * rs, rs


def load_rows(s, m, x_ref, g_ref, seg_ref, blk):
    start = start_of(seg_ref[m : m + 1, :])
    rows = slice(m * blk, (m + 1) * blk)
    diff = iota((blk, blk), 1) - iota((blk, blk), 0)
    perm = one_hot((diff == start) | (diff == start - blk))
    both = jnp.concatenate([x_ref[rows, :], g_ref[rows, :]], axis=1)
    rolled = dot_n(perm, both).astype(BF16)
    unit = eye()
    s.out[m] = dot_t(unit, rolled[:, 0:D])
    s.gt[m] = dot_t(unit, rolled[:, D : 2 * D]).astype(BF16)
    for at in range(0, blk, 128):
        cs = slice(at, at + 128)
        vhat, rs = norm_of(s.out[m, :, cs])
        s.vh1[m, :, cs] = vhat
        s.rs1[m, :, cs] = jnp.broadcast_to(rs, (8, 128))
        add_to(s, AB2, m + at, s.gt[m, :, cs].astype(F32))
    seg = seg_ref[m : m + 1, :].astype(F32).astype(BF16)
    tail = perm[blk // 2 :, :]
    seg_row = dot_t(jnp.broadcast_to(seg, (16, blk)), tail)[0:1, :]
    seg_col = dot_t(tail, jnp.broadcast_to(seg, (128, blk)))
    bias = jnp.where(wide_of(seg_col, blk // 2) == seg_row, 0.0, -1e30)
    s.bias[m] = bias.astype(BF16)


def project(s, m, blk):
    for at in range(0, blk, 128):
        cs = slice(at, at + 128)
        a = s.vh1[m, :, cs] * s.col[OG1 : OG1 + D].astype(F32) + s.col[OC1 : OC1 + D].astype(F32)
        s.at[m, :, cs] = a.astype(BF16)
    qkv = dot_n(s.wqkvt[...], s.at[m])
    q = (qkv[0:D] + col_of(s, OBQ, blk)).astype(BF16)
    s.qt[m] = q * jnp.asarray(HD ** (-0.5), BF16)
    k = qkv[D : 2 * D].astype(BF16)
    v = (qkv[2 * D :] + col_of(s, OBV, blk)).astype(BF16)
    s.kt[m] = k
    s.vt[m] = v
    unit = eye()
    for at in range(0, blk, D):
        s.dqkv[m % 2, at : at + D, m // 2 * D : m // 2 * D + D] = dot_t(unit, k[:, at : at + D]).astype(BF16)
        s.vn[m, at : at + D, :] = dot_t(unit, v[:, at : at + D]).astype(BF16)


def pair_rows(v, head):
    zero = jnp.zeros_like(v)
    return jnp.concatenate([v, zero] if head % 2 == 0 else [zero, v], axis=0)


def unit_of(i, blk):
    half = blk // 2
    m, part, head = i // (2 * HEADS), i // HEADS % 2, i % HEADS
    qs = slice(part * half, (part + 1) * half)
    hr = slice(head * HD, (head + 1) * HD)
    pc = slice(head // 2 * 128, head // 2 * 128 + 128)
    return m, part, head, qs, hr, pc


def pipeline(units, pre, mid, post, extra):
    for i in range(-1, units + 1):
        if i + 1 < units:
            pre(i + 1)
        if 0 <= i < units:
            mid(i)
        if i >= 1:
            post(i - 1)
        for call in extra.get(i, ()):
            call()


def attend(s, mb, blk, extra):
    half = blk // 2

    def pre(i):
        m, part, head, qs, hr, pc = unit_of(i, blk)
        keys = s.dqkv[m % 2, qs, m // 2 * D + pc.start : m // 2 * D + pc.stop]
        s.hs[i % 2, 0:half, 0:half] = dot_n(keys, pair_rows(s.qt[m, hr, qs], head))

    def mid(i):
        m, part, head, qs, hr, pc = unit_of(i, blk)
        for at in range(0, half, 128):
            cs = slice(at, at + 128)
            st = s.hs[i % 2, 0:half, cs]
            if part == 1:
                st = st + s.bias[m, :, cs].astype(F32)
            e = jnp.exp(st - jnp.max(st, axis=0, keepdims=True))
            prob = e * (1.0 / jnp.sum(e, axis=0, keepdims=True))
            s.prob[m, part, head, :, cs] = prob.astype(BF16)

    def post(i):
        m, part, head, qs, hr, pc = unit_of(i, blk)
        s.ot[m, hr, qs] = dot_n(s.vt[m, hr, qs], s.prob[m, part, head]).astype(BF16)

    pipeline(mb * 2 * HEADS, pre, mid, post, extra)


def middle(s, m, blk):
    s.dz[m % 2, 0:D, :] = dot_n(s.wot[...], s.ot[m])
    s.bt[m, D:, :] = jnp.ones((16, blk), BF16)
    for at in range(0, blk, 128):
        cs = slice(at, at + 128)
        y = s.out[m, :, cs] + s.dz[m % 2, 0:D, cs] + s.col[OBO : OBO + D].astype(F32)
        vhat, rs = norm_of(y)
        s.vh2[m, :, cs] = vhat
        s.rs2[m, :, cs] = jnp.broadcast_to(rs, (8, 128))
        s.bt[m, 0:D, cs] = (vhat * s.col[OG2 : OG2 + D].astype(F32) + s.col[OC2 : OC2 + D].astype(F32)).astype(BF16)
        s.out[m, :, cs] = y + s.col[OB2 : OB2 + D].astype(F32)


def feed_forward(s, mb, blk, fc=512, br=32, first=0, last=FF // 512):
    def pre(c, m, p):
        cs = pl.ds(pl.multiple_of(c * fc, fc), fc)
        s.hs[p] = dot_n(s.w1t[cs, :], s.bt[m, 0:D, :])
        s.dz[p] = dot_n(s.w2[cs, :], s.gt[m])

    def mid(c, m, p):
        for r in range(0, fc, br):
            rs = slice(r, r + br)
            bias = s.col[pl.ds(pl.multiple_of(OB1 + c * fc + r, br), br), :].astype(F32)
            z, slope = gelu_both(s.hs[p, rs, :] + wide_of(bias, blk))
            s.zb[p, rs, :] = z.astype(BF16)
            s.dh[p, rs, :] = (s.dz[p, rs, :] * slope).astype(BF16)

    def post(c, m, p):
        cs = pl.ds(pl.multiple_of(c * fc, fc), fc)
        z, dh = s.zb[p], s.dh[p]
        s.out[m] = s.out[m] + dot_n(s.w2t[:, cs], z)
        d = dot_n(s.w1[:, cs], dh)
        s.db[m] = s.db[m] + d
        g2 = dot_t(z, s.gt[m])
        g1 = dot_t(s.bt[m], dh)
        s.g2[cs, :] = g2 if m == 0 else s.g2[cs, :] + g2
        s.g1[:, cs] = g1 if m == 0 else s.g1[:, cs] + g1

    if first == 0:
        for m in range(mb):
            s.db[m] = jnp.zeros((D, blk), F32)
        pre(0, 0, 0)

    def block(c, carry):
        for m in range(mb):
            if m + 1 < mb:
                pre(c, m + 1, (m + 1) % 2)
            else:
                pre(jnp.minimum(c + 1, FF // fc - 1), 0, 0)
            mid(c, m, m % 2)
            if m > 0:
                post(c, m - 1, (m - 1) % 2)
        post(c, mb - 1, (mb - 1) % 2)
        return carry

    lax.fori_loop(first, last, block, 0)


def norm_back(u, vhat, rs, gain):
    gu = u * gain
    return (gu - col_mean(gu) - vhat * col_mean(gu * vhat)) * rs


def add_to(s, which, first, value):
    s.acc[which] = value if first == 0 else s.acc[which] + value


def unroll_rows(m, value, seg_ref, ref, blk):
    start = start_of(seg_ref[m : m + 1, :])
    diff = iota((blk, blk), 0) - iota((blk, blk), 1)
    perm = one_hot((diff == start) | (diff == start - blk))
    ref[m * blk : (m + 1) * blk, :] = dot_t(perm, value).astype(BF16)


def back_middle(s, m, seg_ref, out_ref, blk):
    unroll_rows(m, s.out[m].astype(BF16), seg_ref, out_ref, blk)
    for at in range(0, blk, 128):
        cs = slice(at, at + 128)
        u = s.db[m, :, cs]
        vhat = s.vh2[m, :, cs]
        add_to(s, AG2, m + at, u * vhat)
        add_to(s, AC2, m + at, u)
        back = norm_back(u, vhat, s.rs2[m, 0:1, cs], s.col[OG2 : OG2 + D].astype(F32))
        dy = s.gt[m, :, cs].astype(F32) + back
        s.out[m, :, cs] = dy
        add_to(s, ABO, m + at, dy)
        s.zb[m % 2, D:, cs] = dy.astype(BF16)
    dp = s.zb[m % 2, D:, :]
    gwo = dot_t(s.ot[m], dp)
    s.ga[:, 3 * D :] = gwo if m == 0 else s.ga[:, 3 * D :] + gwo
    s.bt[m, 0:D, :] = dot_n(s.wo[...], dp).astype(BF16)


def back_attend(s, mb, blk, extra):
    half = blk // 2
    scale = HD ** (-0.5)

    def pre(i):
        m, part, head, qs, hr, pc = unit_of(i, blk)
        s.hs[i % 2, 0:half, 0:half] = dot_n(s.vn[m, qs, pc], pair_rows(s.bt[m, hr, qs], head))

    def mid(i):
        m, part, head, qs, hr, pc = unit_of(i, blk)
        for at in range(0, half, 128):
            cs = slice(at, at + 128)
            prob = s.prob[m, part, head, :, cs].astype(F32)
            weighted = prob * s.hs[i % 2, 0:half, cs]
            ds = weighted - prob * jnp.sum(weighted, axis=0, keepdims=True)
            s.zb[i % 2, 0:half, cs] = ds.astype(BF16)

    def post(i):
        m, part, head, qs, hr, pc = unit_of(i, blk)
        ds = s.zb[i % 2, 0:half, 0:half]
        dq = dot_n(s.kt[m, hr, qs], ds) * scale
        dk = dot_t(s.qt[m, hr, qs], ds)
        dv = dot_t(s.bt[m, hr, qs], s.prob[m, part, head])
        for c, value in enumerate((dq, dk, dv)):
            at = c * D + head * HD
            s.dqkv[m % 2, at : at + HD, qs] = value.astype(BF16)

    pipeline(mb * 2 * HEADS, pre, mid, post, extra)


def back_project(s, m, seg_ref, dx_ref, blk):
    dqkv = s.dqkv[m % 2]
    s.dz[m % 2, 0:D, :] = dot_n(s.wcat[...], dqkv)
    g = dot_t(s.at[m], dqkv)
    s.ga[:, 0 : 3 * D] = g if m == 0 else s.ga[:, 0 : 3 * D] + g
    for at in range(0, blk, 128):
        cs = slice(at, at + 128)
        add_to(s, ABQ, m + at, s.dqkv[m % 2, 0:D, cs].astype(F32))
        add_to(s, ABV, m + at, s.dqkv[m % 2, 2 * D :, cs].astype(F32))
        u = s.dz[m % 2, 0:D, cs]
        vhat = s.vh1[m, :, cs]
        add_to(s, AG1, m + at, u * vhat)
        add_to(s, AC1, m + at, u)
        back = norm_back(u, vhat, s.rs1[m, 0:1, cs], s.col[OG1 : OG1 + D].astype(F32))
        s.dh[m % 2, D:, cs] = (s.out[m, :, cs] + back).astype(BF16)
    unroll_rows(m, s.dh[m % 2, D:, :], seg_ref, dx_ref, blk)


def vector_row(s):
    ones = jnp.ones((16, 128), BF16)
    rows = []
    for which in range(8):
        v = s.acc[which]
        high = v.astype(BF16)
        low = (v - high.astype(F32)).astype(BF16)
        rows.append((dot_t(ones, high) + dot_t(ones, low))[0:8, :])
    return jnp.concatenate(rows + [s.g1[D : D + 8, :]], axis=1)


class Names:
    def __init__(self, keys, refs):
        for key, ref in zip(keys, refs):
            setattr(self, key, ref)


class Place:
    def __init__(self):
        wide = lax.axis_index("wide")
        narrow = lax.axis_index("narrow")
        self.z, self.y = lax.div(wide, 2), lax.rem(wide, 2)
        self.x, self.core = lax.div(narrow, 2), lax.rem(narrow, 2)

    def along(self, kind, k):
        if kind == "z":
            z = lax.rem(self.z + k, 4)
            return z, (z * 2 + self.y, self.x * 2 + self.core)
        x = self.x + (k % 2) * (1 - 2 * self.x)
        y = self.y + (k // 2) * (1 - 2 * self.y)
        return y * 2 + x, (self.z * 2 + y, x * 2 + self.core)

    def sibling(self):
        return (self.z * 2 + self.y, self.x * 2 + 1 - self.core)


def device_at(z, plane, core):
    return z * 8 + plane * 2 + core


def slot_of(device):
    return device % 2 * 16 + device // 2 % 4 * 4 + device // 8


def remote(src, dst, send, recv, device):
    return pltpu.make_async_remote_copy(
        src_ref=src, dst_ref=dst, send_sem=send, recv_sem=recv, device_id=device, device_id_type=MESH
    )


def greet(place):
    barrier = pltpu.get_barrier_semaphore()
    partners = [place.along(kind, k)[1] for kind in ("z", "plane") for k in (1, 2, 3)]
    partners.append(place.sibling())
    for partner in partners:
        pl.semaphore_signal(barrier, inc=1, device_id=partner, device_id_type=MESH)
    pl.semaphore_wait(barrier, len(partners))


class Gather:
    def __init__(self, place, buf, send, recv):
        base = place.core * 16
        group = base + place.along("plane", 0)[0] * 4
        self.own = group + place.z
        self.first, self.second, self.third = [], [], []
        for k in (1, 2, 3):
            at = buf.at[self.own]
            to = place.along("z", k)[1]
            self.first.append(remote(at, at, send.at[k - 1], recv.at[k - 1], to))
            at = buf.at[pl.ds(group, 4)]
            to = place.along("plane", k)[1]
            self.second.append(remote(at, at, send.at[2 + k], recv.at[2 + k], to))
        for k in range(4):
            at = buf.at[pl.ds(base + place.along("plane", k)[0] * 4, 4)]
            self.third.append(remote(at, at, send.at[6 + k], recv.at[6 + k], place.sibling()))

    def start_first(self):
        for copy in self.first:
            copy.start()

    def start_second(self):
        for copy in self.first:
            copy.wait_recv()
        for copy in self.second:
            copy.start()
        self.third[0].start()

    def start_third(self):
        for copy, after in zip(self.second, self.third[1:]):
            copy.wait_recv()
            after.start()

    def finish(self):
        for copy in self.third:
            copy.wait_recv()
        for copy in self.first + self.second + self.third:
            copy.wait_send()


class Scatter:
    def __init__(self, place, line, own, done, buf, got, held, send, recv):
        self.place, self.line, self.own, self.done = place, line, own, done
        self.buf, self.got, self.held = buf, got, held
        n = len(line)
        self.first, self.second, self.third = [], [], []
        for k in range(4):
            at = pl.ds(place.along("plane", k)[0] * n, n)
            self.first.append(
                remote(buf.at[at], got.at[at], send.at[k], recv.at[k], place.sibling())
            )
        for k in (1, 2, 3):
            at = pl.ds((3 + k) * n, n)
            to = place.along("plane", k)[1]
            self.second.append(
                remote(buf.at[at], got.at[at], send.at[3 + k], recv.at[3 + k], to)
            )
            at = 7 * n + k - 1
            to = place.along("z", k)[1]
            self.third.append(
                remote(buf.at[at], got.at[at], send.at[6 + k], recv.at[6 + k], to)
            )

    def owned(self, z, call):
        if len(self.line) == 4:
            call()
        else:
            pl.when((z >= self.line[0]) & (z <= self.line[-1]))(call)

    def start_first(self):
        n = len(self.line)
        for plane in range(4):
            for j, z in enumerate(self.line):
                term = self.own(device_at(z, plane, 1 - self.place.core))
                self.buf[plane * n + j] = term.astype(BF16)
        for k in (3, 1, 2, 0):
            self.first[k].start()

    def start_second(self):
        n = len(self.line)
        for k in (3, 1, 2, 0):
            self.first[k].wait_recv()
            plane = self.place.along("plane", k)[0]
            for j, z in enumerate(self.line):
                term = self.own(device_at(z, plane, self.place.core))
                term = term + self.got[plane * n + j].astype(F32)
                if k == 0:
                    self.held[j] = term
                else:
                    self.buf[(3 + k) * n + j] = term.astype(BF16)
            if k > 0:
                self.second[k - 1].start()

    def start_third(self):
        n = len(self.line)
        for copy in self.second:
            copy.wait_recv()
        for j in range(n):
            term = self.held[j]
            for k in (1, 2, 3):
                term = term + self.got[(3 + k) * n + j].astype(F32)
            self.held[j] = term
        for k in (1, 2, 3):
            z = self.place.along("z", k)[0]

            def send(k=k, z=z):
                self.buf[7 * n + k - 1] = self.held[z - self.line[0]].astype(BF16)
                self.third[k - 1].start()

            self.owned(z, send)

    def finish(self):
        n = len(self.line)

        def take():
            term = self.held[self.place.z - self.line[0]]
            for k in (1, 2, 3):
                self.third[k - 1].wait_recv()
                term = term + self.got[7 * n + k - 1].astype(F32)
            self.done(term)

        self.owned(self.place.z, take)
        for copy in self.first + self.second:
            copy.wait_send()
        for k in (1, 2, 3):
            self.owned(self.place.along("z", k)[0], self.third[k - 1].wait_send)


def entry_place(k):
    gain, rest = k < 512.0, k - 512.0
    device = jnp.where(gain, jnp.floor((k + 0.5) * (1.0 / 16)), jnp.floor((rest + 0.5) * (1.0 / 112)))
    lane = jnp.where(gain, k - 16.0 * device, rest - 112.0 * device + 16.0)
    return device, lane


def pick_at(s, at):
    ref = s.w1t if at < FF else s.w2
    return ref.at[at % FF : at % FF + 512]


def make_tables(s):
    row = iota((8, 256), 1)
    slot = row // 8
    device = slot % 4 * 8 + slot // 4 % 4 * 2 + slot // 16
    first_gain = jnp.where(row % 8 == 0, 16 * device, 8192)[0:1, :]
    first_bias = jnp.where(row % 8 == 0, 512 + 112 * device, 8192)[0:1, :]
    for at in range(0, NVEC, 512):
        k = iota((512, 256), 0) + at
        first, count = (first_gain, 16) if at < 512 else (first_bias, 112)
        pick_at(s, at)[...] = one_hot((k >= first) & (k < first + count))
        _, lane = entry_place((iota((512, 128), 0) + at).astype(F32))
        s.keep[at : at + 512, :] = one_hot(lane == iota((512, 128), 1).astype(F32))
    device, _ = entry_place(iota((16, NVEC), 1).astype(F32))
    for at in (0, 16):
        s.mine[at : at + 16, :] = one_hot(device == (iota((16, NVEC), 0) + at).astype(F32))


def unpack_attention(s):
    for c in range(4):
        rows = [s.bufa[slot_of(d), 8 * c : 8 * c + 8, :].astype(F32) for d in range(32)]
        full = jnp.concatenate(rows, axis=0).astype(BF16)
        if c < 3:
            s.wcat[:, c * D : (c + 1) * D] = full
        else:
            s.wo[...] = full
    rows = [s.bufa[d, 32:40, 0:128].astype(F32) for d in range(32)]
    table = jnp.concatenate(rows, axis=0).astype(BF16)
    ones = jnp.ones((128, 128), BF16)
    for at in range(0, NVEC, 512):
        found = dot_n(pick_at(s, at)[...], table).astype(BF16) * s.keep[at : at + 512, :]
        s.col[at : at + 512, :] = dot_n(found, ones).astype(BF16)


def unpack_inner(s):
    for i in range(16):
        pair = [s.buf1[slot_of(2 * i + c)].astype(F32) for c in range(2)]
        for h in range(2):
            rows = jnp.concatenate([v[8 * h : 8 * h + 8] for v in pair], axis=0)
            s.w1[16 * i : 16 * i + 16, h * FF // 2 : (h + 1) * FF // 2] = rows.astype(BF16)
    for d in range(32):
        s.w2[64 * d : 64 * d + 64, :] = s.buf2[slot_of(d)]


def vector_rows(s):
    row = vector_row(s)[0:1, :]
    high = row.astype(BF16).astype(F32)
    total = None
    for term in (high, row - high):
        part = dot_n((s.mine[...].astype(F32) * term).astype(BF16), s.keep[...])
        total = part if total is None else total + part
    high = total.astype(BF16).astype(F32)
    s.vrow[:, 0:128] = high
    s.vrow[:, 128:256] = total - high


def fold(rows):
    half = rows.shape[1] // 2
    return jnp.concatenate([rows[:, :half], rows[:, half:]], axis=0)


def own_attention(s):
    def load(device):
        rows = pl.ds(pl.multiple_of(device * 8, 8), 8)
        parts = [s.ga[rows, c * D : (c + 1) * D] for c in range(4)]
        vector = jnp.broadcast_to(s.vrow[pl.ds(device, 1), :], (8, D))
        return jnp.concatenate(parts + [vector], axis=0)

    return load


def own_first(s, half):
    cols = slice(half * (FF // 2), (half + 1) * (FF // 2))
    return lambda device: fold(s.g1[pl.ds(pl.multiple_of(device * 8, 8), 8), cols])


def own_second(s):
    return lambda device: s.g2[pl.ds(pl.multiple_of(device * 64, 64), 64), :]


MSG = 40
SUMS = {
    "a": (4, MSG, D),
    "1x": (4, 16, FF // 4),
    "1y": (4, 16, FF // 4),
    "2x": (2, 64, D),
    "2y": (2, 64, D),
}


def fused_scratch(mb, blk):
    shapes = scratch_shapes(mb, blk)
    for name, (rows, cols) in (("a", (MSG, D)), ("1", (16, FF // 2)), ("2", (64, D))):
        shapes["buf" + name] = pltpu.VMEM((32, rows, cols), BF16)
        shapes["gsend" + name] = pltpu.SemaphoreType.DMA((10,))
        shapes["grecv" + name] = pltpu.SemaphoreType.DMA((10,))
    for name, (n, rows, cols) in SUMS.items():
        if name != "2x":
            shapes["out" + name] = pltpu.VMEM((7 * n + 3, rows, cols), BF16)
        shapes["got" + name] = pltpu.VMEM((7 * n + 3, rows, cols), BF16)
        shapes["held" + name] = pltpu.VMEM((n, rows, cols), F32)
        shapes["ssend" + name] = pltpu.SemaphoreType.DMA((10,))
        shapes["srecv" + name] = pltpu.SemaphoreType.DMA((10,))
    shapes["keep"] = pltpu.VMEM((NVEC, 128), BF16)
    shapes["mine"] = pltpu.VMEM((32, NVEC), BF16)
    shapes["vrow"] = pltpu.VMEM((32, D), F32)
    shapes["line"] = pltpu.VMEM((8, D), F32)
    for name in ("xs", "gs"):
        shapes[name] = pltpu.VMEM((mb * blk, D), BF16)
    shapes["insem"] = pltpu.SemaphoreType.DMA((2,))
    shapes["outsem"] = pltpu.SemaphoreType.DMA((2 * mb,))
    return shapes


def fused_kernel(keys, mb, blk, *refs):
    x_hbm, seg_ref, g_hbm, wa, w1, w2, gains, biases = refs[:8]
    out_hbm, dx_hbm, suma, sum1, sum2 = refs[8:13]
    s = Names(keys, refs[13:])
    place = Place()
    loads = []
    for i, (hbm, ref) in enumerate(((x_hbm, s.xs), (g_hbm, s.gs))):
        loads.append(pltpu.make_async_copy(hbm, ref, s.insem.at[i]))
        loads[-1].start()
    gather = {
        n: Gather(place, getattr(s, "buf" + n), getattr(s, "gsend" + n), getattr(s, "grecv" + n))
        for n in "a12"
    }
    s.line[...] = jnp.zeros((8, D), F32)
    s.line[0:1, 0:16] = gains[...]
    s.line[0:1, 16:128] = biases[...]
    own = jnp.concatenate([wa[c] for c in range(4)] + [s.line[...]], axis=0).astype(BF16)
    s.bufa[gather["a"].own] = own
    s.buf1[gather["1"].own] = fold(w1[...]).astype(BF16)
    s.buf2[gather["2"].own] = w2[...].astype(BF16)
    greet(place)
    gather["a"].start_first()
    make_tables(s)
    gather["a"].start_second()
    gather["1"].start_first()
    gather["2"].start_first()
    for copy in loads:
        copy.wait()
    for m in range(mb):
        load_rows(s, m, s.xs, s.gs, seg_ref, blk)
    gather["a"].start_third()
    gather["1"].start_second()
    gather["2"].start_second()
    gather["a"].finish()
    unpack_attention(s)
    transpose_weights_attention(s)
    project(s, 0, blk)
    project(s, 1, blk)
    extra = {}

    def at(step, f, *args):
        extra.setdefault(step, []).append(functools.partial(f, *args))

    for m in range(mb):
        if m + 2 < mb:
            at(8 * m + 4, project, s, m + 2, blk)
        at(8 * m + 8, middle, s, m, blk)
    at(20, gather["1"].start_third)
    at(20, gather["2"].start_third)
    attend(s, mb, blk, extra)
    gather["1"].finish()
    gather["2"].finish()
    unpack_inner(s)
    transpose_weights_inner(s)
    scatter = {}
    s.out2x = s.buf2.at[0:17]

    def sum_into(name, line, own, done):
        refs = [getattr(s, key + name) for key in ("out", "got", "held", "ssend", "srecv")]
        scatter[name] = Scatter(place, line, own, done, *refs)

    def into(ref):
        def store(value):
            ref[...] = value

        return store

    def into_first(half):
        def store(value):
            for part in range(2):
                at = (2 * half + part) * FF // 4
                sum1[:, at : at + FF // 4] = value[8 * part : 8 * part + 8]

        return store

    sum_into("a", range(4), own_attention(s), into(suma))
    for half, name in enumerate("xy"):
        sum_into("1" + name, range(4), own_first(s, half), into_first(half))
        sum_into("2" + name, range(2 * half, 2 * half + 2), own_second(s), into(sum2))
    feed_forward(s, mb, blk, first=0, last=2)
    scatter["1x"].start_first()
    scatter["2x"].start_first()
    feed_forward(s, mb, blk, first=2, last=3)
    scatter["1x"].start_second()
    scatter["2x"].start_second()
    feed_forward(s, mb, blk, first=3, last=4)
    scatter["1y"].start_first()
    scatter["2y"].start_first()
    scatter["1x"].start_third()
    scatter["2x"].start_third()
    saves = []

    def save(m, ref, hbm, kind):
        rows = pl.ds(m * blk, blk)
        saves.append(pltpu.make_async_copy(ref.at[rows], hbm.at[rows], s.outsem.at[2 * m + kind]))
        saves[-1].start()

    back_middle(s, 0, seg_ref, s.xs, blk)
    save(0, s.xs, out_hbm, 0)
    extra.clear()
    for m in range(mb):
        if m + 1 < mb:
            at(8 * m + 3, back_middle, s, m + 1, seg_ref, s.xs, blk)
            at(8 * m + 3, save, m + 1, s.xs, out_hbm, 0)
        at(8 * m + 8, back_project, s, m, seg_ref, s.gs, blk)
        at(8 * m + 8, save, m, s.gs, dx_hbm, 1)
    at(8, scatter["1y"].start_second)
    at(8, scatter["2y"].start_second)
    at(25, scatter["1x"].finish)
    at(25, scatter["2x"].finish)
    at(25, scatter["1y"].start_third)
    at(25, scatter["2y"].start_third)
    back_attend(s, mb, blk, extra)
    vector_rows(s)
    scatter["a"].start_first()
    scatter["1y"].finish()
    scatter["2y"].finish()
    scatter["a"].start_second()
    scatter["a"].start_third()
    for copy in saves:
        copy.wait()
    scatter["a"].finish()


STEP = 10
BETA_ONE = 0.9
BETA_TWO = 0.999
ADAM_EPS = 1e-08
RATES = (0.08, 0.08, 0.08, 0.6, 0.6)
DECAYS = (0.01, 0.01, 0.01, 0.0, 0.0)


def adamw(weight, grad, first, second, rate, decay):
    first_new = BETA_ONE * first + (1.0 - BETA_ONE) * grad
    second_new = BETA_TWO * second + (1.0 - BETA_TWO) * grad * grad
    first_hat = first_new / (1.0 - BETA_ONE**STEP)
    second_hat = second_new / (1.0 - BETA_TWO**STEP)
    weight_new = weight - rate * (first_hat / (jnp.sqrt(second_hat) + ADAM_EPS) + decay * weight)
    return weight_new, first_new, second_new


def adam_kernel(*refs):
    suma, sum1, sum2 = refs[:3]
    state, rows, new, saved, sem = refs[3:18], refs[18:20], refs[20:35], refs[35:37], refs[38]
    held = refs[37]
    step = rows[0].shape[0] // 4
    pieces = [(i, pl.ds(j * step, step)) for i in range(2) for j in range(4)]
    copies = []
    for n, (i, at) in enumerate(pieces):
        copies.append(pltpu.make_async_copy(rows[i].at[at], held.at[i, at], sem.at[n]))
        copies[-1].start()
    for n, (i, at) in enumerate(pieces):
        copies[n].wait()
        copies[n] = pltpu.make_async_copy(held.at[i, at], saved[i].at[at], sem.at[8 + n])
        copies[n].start()

    def update(member, grad, at=()):
        at = at if at else (slice(None),)
        values = adamw(
            state[member][at], grad, state[5 + member][at], state[10 + member][at], RATES[member], DECAYS[member]
        )
        for kind in range(3):
            new[5 * kind + member][at] = values[kind]

    for c in range(4):
        update(0, suma[8 * c : 8 * c + 8, :], (c,))
    update(1, sum1[...])
    update(2, sum2[...])
    line = suma[32:33, 0:128] + suma[32:33, 128:256]
    update(3, line[:, 0:16])
    update(4, line[:, 16:128])
    for copy in copies:
        copy.wait()


VMEM_SPEC = pl.BlockSpec(memory_space=pltpu.VMEM)
ANY_SPEC = pl.BlockSpec(memory_space=pl.ANY)


def fused_device(*args):
    frames, segments, out_grad = args[:3]
    rows = lambda v: v.reshape(1, -1) if v.ndim == 1 else v
    state = [rows(v) for v in args[3:]]
    mb, blk = segments.shape
    shapes = fused_scratch(mb, blk)
    like = lambda v: jax.ShapeDtypeStruct(v.shape, v.dtype)
    out, dx, suma, sum1, sum2 = pl.pallas_call(
        functools.partial(fused_kernel, list(shapes), mb, blk),
        out_shape=[like(frames), like(frames)]
        + [jax.ShapeDtypeStruct(t, F32) for t in ((MSG, D), (8, FF), (64, D))],
        in_specs=[ANY_SPEC, VMEM_SPEC, ANY_SPEC] + [VMEM_SPEC] * 5,
        out_specs=[ANY_SPEC] * 2 + [VMEM_SPEC] * 3,
        scratch_shapes=list(shapes.values()),
        compiler_params=pltpu.CompilerParams(
            collective_id=0, has_side_effects=True, vmem_limit_bytes=63 * 2**20
        ),
    )(frames, segments, out_grad, *state[:5])
    *new, out, dx = pl.pallas_call(
        adam_kernel,
        out_shape=[like(v) for v in state] + [like(out), like(dx)],
        in_specs=[VMEM_SPEC] * 18 + [ANY_SPEC] * 2,
        out_specs=[VMEM_SPEC] * 15 + [ANY_SPEC] * 2,
        scratch_shapes=[pltpu.VMEM((2, *out.shape), BF16), pltpu.SemaphoreType.DMA((16,))],
    )(suma, sum1, sum2, *state, out, dx)
    return (out, dx, *[v.reshape(t.shape) for v, t in zip(new, args[3:])])


def local_kernel(keys, mb, blk, *refs):
    x_ref, seg_ref, g_ref, wa, w1, w2, col = refs[:7]
    out_ref, dx_ref, ga, g1, g2, gv = refs[7:13]
    s = Names(keys, refs[13:])
    for c in range(3):
        s.wcat[:, c * D : (c + 1) * D] = wa[c]
    s.wo[...] = wa[3]
    s.w1[...] = w1[...]
    s.w2[...] = w2[...]
    s.col[...] = col[...].astype(BF16)
    transpose_weights_attention(s)
    transpose_weights_inner(s)
    for m in range(mb):
        load_rows(s, m, x_ref, g_ref, seg_ref, blk)
        project(s, m, blk)
    attend(s, mb, blk, {})
    for m in range(mb):
        middle(s, m, blk)
    feed_forward(s, mb, blk)
    extra = {}
    for m in range(mb):
        back_middle(s, m, seg_ref, out_ref, blk)
        extra[8 * m + 8] = [functools.partial(back_project, s, m, seg_ref, dx_ref, blk)]
    back_attend(s, mb, blk, extra)
    gv[...] = vector_row(s)
    ga[...] = s.ga[...]
    g1[...] = s.g1[0:D, :]
    g2[...] = s.g2[...]


AXES = ("wide", "narrow")


def local_device(*args):
    frames, segments, out_grad = args[:3]
    weights, firsts, seconds = args[3:8], args[8:13], args[13:18]
    dims = (1, 0, 0, 0, 0)
    full = [
        lax.all_gather(w.astype(BF16), AXES, axis=dim, tiled=True) for w, dim in zip(weights, dims)
    ]
    mb, blk = segments.shape
    table = jnp.concatenate([full[3], full[4]]).astype(F32)
    shapes = scratch_shapes(mb, blk)
    like = lambda v: jax.ShapeDtypeStruct(v.shape, v.dtype)
    out, dx, ga, g1, g2, gv = pl.pallas_call(
        functools.partial(local_kernel, list(shapes), mb, blk),
        out_shape=[like(frames), like(frames)]
        + [jax.ShapeDtypeStruct(t, F32) for t in ((D, 4 * D), (D, FF), (FF, D), (8, NVEC))],
        in_specs=[VMEM_SPEC] * 7,
        out_specs=[VMEM_SPEC] * 6,
        scratch_shapes=list(shapes.values()),
        compiler_params=pltpu.CompilerParams(vmem_limit_bytes=63 * 2**20),
    )(frames, segments, out_grad, *full[:3], jnp.broadcast_to(table[:, None], (NVEC, 128)))
    grads = (jnp.stack(jnp.split(ga, 4, axis=1)), g1, g2, gv[0, :512], gv[0, 512:])
    owned = [
        lax.psum_scatter(g, AXES, scatter_dimension=dim, tiled=True) for g, dim in zip(grads, dims)
    ]
    new = [adamw(*v) for v in zip(weights, owned, firsts, seconds, RATES, DECAYS)]
    return (out, dx, *[new[member][kind] for kind in range(3) for member in range(5)])


def solution(mesh):
    rows, matrix, vector = P(AXES, None), P(None, AXES, None), P(AXES)
    group = (matrix, rows, rows, vector, vector)
    fits = (mesh.shape["wide"], mesh.shape["narrow"]) == (8, 4)
    return jax.shard_map(
        fused_device if fits else local_device,
        mesh=mesh,
        in_specs=(rows, rows, rows, *group, *group, *group),
        out_specs=(rows, rows, *group, *group, *group),
        check_vma=False,
    )
```

```python
import functools
import jax
import jax.numpy as jnp
from jax import lax
from jax.experimental import pallas as pl
from jax.experimental.pallas import tpu as pltpu
from jax.sharding import PartitionSpec as P

D = 256
HEADS = 4
HD = 64
FF = 2048
NORM_EPS = 1e-05
C_ONE = 0.7978845608028654
C_THREE = C_ONE * 0.044715
F32 = jnp.float32
BF16 = jnp.bfloat16


MESH = pl.DeviceIdType.MESH


def dot_n(a, b):
    return jnp.dot(a, b, preferred_element_type=F32)


def dot_t(a, b):
    return lax.dot_general(a, b, (((1,), (1,)), ((), ())), preferred_element_type=F32)


def iota(shape, dim):
    return lax.broadcasted_iota(jnp.int32, shape, dim)


def one_hot(cond):
    return jnp.where(cond, 1.0, 0.0).astype(BF16)


def eye():
    return one_hot(iota((D, D), 0) == iota((D, D), 1))


def wide_of(col, width):
    return jnp.concatenate([col] * (width // 128), axis=1)


def lane_fold(v):
    total = v[:, 0:128]
    for at in range(128, v.shape[1], 128):
        total = total + v[:, at : at + 128]
    return total


def col_mean(v):
    return jnp.sum(v, axis=0, keepdims=True) * (1.0 / v.shape[0])


def start_of(seg):
    start = jnp.full((1, 1), 4096.0, F32)
    for v in range(4):
        count = jnp.sum(jnp.where(seg == v, 1.0, 0.0), axis=1, keepdims=True)
        below = jnp.sum(jnp.where(seg < v, 1.0, 0.0), axis=1, keepdims=True)
        start = jnp.minimum(start, jnp.where(count == 256.0, below, 4096.0))
    return start.astype(jnp.int32)


def gelu_both(h):
    h2 = h * h
    t = jnp.tanh(h * (C_THREE * h2 + C_ONE))
    s = 0.5 * t + 0.5
    z = h * s
    slope = s + z * (1.0 - s) * (6.0 * C_THREE * h2 + 2.0 * C_ONE)
    return z, slope


OG1, OG2, OBQ, OBV, OBO, OB2, OC1, OC2, OB1 = 0, 256, 512, 768, 1024, 1280, 1536, 1792, 2048
NVEC = 4096
AG1, AG2, ABQ, ABV, ABO, AB2, AC1, AC2 = range(8)


def scratch_shapes(mb, blk):
    half = blk // 2
    return dict(
        wqkvt=pltpu.VMEM((3 * D, D), BF16),
        wcat=pltpu.VMEM((D, 3 * D), BF16),
        wo=pltpu.VMEM((D, D), BF16),
        wot=pltpu.VMEM((D, D), BF16),
        w1=pltpu.VMEM((D, FF), BF16),
        w1t=pltpu.VMEM((FF, D), BF16),
        w2=pltpu.VMEM((FF, D), BF16),
        w2t=pltpu.VMEM((D, FF), BF16),
        col=pltpu.VMEM((NVEC, 128), BF16),
        vh1=pltpu.VMEM((mb, D, blk), F32),
        rs1=pltpu.VMEM((mb, 8, blk), F32),
        bias=pltpu.VMEM((mb, half, half), BF16),
        vh2=pltpu.VMEM((mb, D, blk), F32),
        rs2=pltpu.VMEM((mb, 8, blk), F32),
        at=pltpu.VMEM((mb, D, blk), BF16),
        bt=pltpu.VMEM((mb, D + 16, blk), BF16),
        gt=pltpu.VMEM((mb, D, blk), BF16),
        qt=pltpu.VMEM((mb, D, blk), BF16),
        kt=pltpu.VMEM((mb, D, blk), BF16),
        vt=pltpu.VMEM((mb, D, blk), BF16),
        vn=pltpu.VMEM((mb, blk, D), BF16),
        ot=pltpu.VMEM((mb, D, blk), BF16),
        prob=pltpu.VMEM((mb, 2, HEADS, half, half), BF16),
        out=pltpu.VMEM((mb, D, blk), F32),
        db=pltpu.VMEM((mb, D, blk), F32),
        hs=pltpu.VMEM((2, 512, blk), F32),
        dz=pltpu.VMEM((2, 512, blk), F32),
        zb=pltpu.VMEM((2, 512, blk), BF16),
        dh=pltpu.VMEM((2, 512, blk), BF16),
        dqkv=pltpu.VMEM((2, 3 * D, blk), BF16),
        acc=pltpu.VMEM((8, D, 128), F32),
        g1=pltpu.VMEM((D + 16, FF), F32),
        g2=pltpu.VMEM((FF, D), F32),
        ga=pltpu.VMEM((D, 4 * D), F32),
    )


def transpose_weights_attention(s):
    unit = eye()
    for c in range(3):
        s.wqkvt[c * D : (c + 1) * D, :] = dot_t(unit, s.wcat[:, c * D : (c + 1) * D]).astype(BF16)
    s.wot[...] = dot_t(unit, s.wo[...]).astype(BF16)


def transpose_weights_inner(s, blocks):
    unit = eye()
    for c in blocks:
        cs = slice(c * D, (c + 1) * D)
        s.w1t[cs, :] = dot_t(unit, s.w1[:, cs]).astype(BF16)
        s.w2t[:, cs] = dot_t(unit, s.w2[cs, :]).astype(BF16)


def col_of(s, at, width):
    return wide_of(s.col[at : at + D, :].astype(F32), width)


def norm_of(v):
    center = v - col_mean(v)
    rs = lax.rsqrt(col_mean(center * center) + NORM_EPS)
    return center * rs, rs


def load_rows(s, m, x_ref, g_ref, seg_ref, blk):
    start = start_of(seg_ref[m : m + 1, :])
    rows = slice(m * blk, (m + 1) * blk)
    diff = iota((blk, blk), 1) - iota((blk, blk), 0)
    perm = one_hot((diff == start) | (diff == start - blk))
    both = jnp.concatenate([x_ref[rows, :], g_ref[rows, :]], axis=1)
    rolled = dot_n(perm, both).astype(BF16)
    unit = eye()
    s.out[m] = dot_t(unit, rolled[:, 0:D])
    s.gt[m] = dot_t(unit, rolled[:, D : 2 * D]).astype(BF16)
    for at in range(0, blk, 128):
        cs = slice(at, at + 128)
        vhat, rs = norm_of(s.out[m, :, cs])
        s.vh1[m, :, cs] = vhat
        s.rs1[m, :, cs] = jnp.broadcast_to(rs, (8, 128))
        add_to(s, AB2, m + at, s.gt[m, :, cs].astype(F32))
    seg = seg_ref[m : m + 1, :].astype(F32).astype(BF16)
    tail = perm[blk // 2 :, :]
    seg_row = dot_t(jnp.broadcast_to(seg, (16, blk)), tail)[0:1, :]
    seg_col = dot_t(tail, jnp.broadcast_to(seg, (128, blk)))
    bias = jnp.where(wide_of(seg_col, blk // 2) == seg_row, 0.0, -1e30)
    s.bias[m] = bias.astype(BF16)


def project(s, m, blk):
    for at in range(0, blk, 128):
        cs = slice(at, at + 128)
        a = s.vh1[m, :, cs] * s.col[OG1 : OG1 + D].astype(F32) + s.col[OC1 : OC1 + D].astype(F32)
        s.at[m, :, cs] = a.astype(BF16)
    qkv = dot_n(s.wqkvt[...], s.at[m])
    q = (qkv[0:D] + col_of(s, OBQ, blk)).astype(BF16)
    s.qt[m] = q * jnp.asarray(HD ** (-0.5), BF16)
    k = qkv[D : 2 * D].astype(BF16)
    v = (qkv[2 * D :] + col_of(s, OBV, blk)).astype(BF16)
    s.kt[m] = k
    s.vt[m] = v
    unit = eye()
    for at in range(0, blk, D):
        s.dqkv[m % 2, at : at + D, m // 2 * D : m // 2 * D + D] = dot_t(unit, k[:, at : at + D]).astype(BF16)
        s.vn[m, at : at + D, :] = dot_t(unit, v[:, at : at + D]).astype(BF16)


def pair_rows(v, head):
    zero = jnp.zeros_like(v)
    return jnp.concatenate([v, zero] if head % 2 == 0 else [zero, v], axis=0)


def unit_of(i, blk):
    half = blk // 2
    m, part, head = i // (2 * HEADS), i // HEADS % 2, i % HEADS
    qs = slice(part * half, (part + 1) * half)
    hr = slice(head * HD, (head + 1) * HD)
    pc = slice(head // 2 * 128, head // 2 * 128 + 128)
    return m, part, head, qs, hr, pc


def pipeline(units, pre, mid, post, extra):
    for i in range(-1, units + 1):
        if i + 1 < units:
            pre(i + 1)
        if 0 <= i < units:
            mid(i)
        if i >= 1:
            post(i - 1)
        for call in extra.get(i, ()):
            call()


def attend(s, mb, blk, extra):
    half = blk // 2

    def pre(i):
        m, part, head, qs, hr, pc = unit_of(i, blk)
        keys = s.dqkv[m % 2, qs, m // 2 * D + pc.start : m // 2 * D + pc.stop]
        s.hs[i % 2, 0:half, 0:half] = dot_n(keys, pair_rows(s.qt[m, hr, qs], head))

    def mid(i):
        m, part, head, qs, hr, pc = unit_of(i, blk)
        for at in range(0, half, 128):
            cs = slice(at, at + 128)
            st = s.hs[i % 2, 0:half, cs]
            if part == 1:
                st = st + s.bias[m, :, cs].astype(F32)
            e = jnp.exp(st - jnp.max(st, axis=0, keepdims=True))
            prob = e * (1.0 / jnp.sum(e, axis=0, keepdims=True))
            s.prob[m, part, head, :, cs] = prob.astype(BF16)

    def post(i):
        m, part, head, qs, hr, pc = unit_of(i, blk)
        s.ot[m, hr, qs] = dot_n(s.vt[m, hr, qs], s.prob[m, part, head]).astype(BF16)

    pipeline(mb * 2 * HEADS, pre, mid, post, extra)


def middle(s, m, blk):
    s.dz[m % 2, 0:D, :] = dot_n(s.wot[...], s.ot[m])
    s.bt[m, D:, :] = jnp.ones((16, blk), BF16)
    for at in range(0, blk, 128):
        cs = slice(at, at + 128)
        y = s.out[m, :, cs] + s.dz[m % 2, 0:D, cs] + s.col[OBO : OBO + D].astype(F32)
        vhat, rs = norm_of(y)
        s.vh2[m, :, cs] = vhat
        s.rs2[m, :, cs] = jnp.broadcast_to(rs, (8, 128))
        s.bt[m, 0:D, cs] = (vhat * s.col[OG2 : OG2 + D].astype(F32) + s.col[OC2 : OC2 + D].astype(F32)).astype(BF16)
        s.out[m, :, cs] = y + s.col[OB2 : OB2 + D].astype(F32)


def feed_forward(s, mb, blk, fc=512, br=32, first=0, last=FF // 512, lead=True, limit=FF // 512, hooks=()):
    def pre(c, m, p):
        cs = pl.ds(pl.multiple_of(c * fc, fc), fc)
        s.hs[p] = dot_n(s.w1t[cs, :], s.bt[m, 0:D, :])
        s.dz[p] = dot_n(s.w2[cs, :], s.gt[m])

    def mid(c, m, p):
        for r in range(0, fc, br):
            rs = slice(r, r + br)
            bias = s.col[pl.ds(pl.multiple_of(OB1 + c * fc + r, br), br), :].astype(F32)
            z, slope = gelu_both(s.hs[p, rs, :] + wide_of(bias, blk))
            s.zb[p, rs, :] = z.astype(BF16)
            s.dh[p, rs, :] = (s.dz[p, rs, :] * slope).astype(BF16)

    def post(c, m, p):
        cs = pl.ds(pl.multiple_of(c * fc, fc), fc)
        z, dh = s.zb[p], s.dh[p]
        s.out[m] = s.out[m] + dot_n(s.w2t[:, cs], z)
        d = dot_n(s.w1[:, cs], dh)
        s.db[m] = s.db[m] + d
        g2 = dot_t(z, s.gt[m])
        g1 = dot_t(s.bt[m], dh)
        s.g2[cs, :] = g2 if m == 0 else s.g2[cs, :] + g2
        s.g1[:, cs] = g1 if m == 0 else s.g1[:, cs] + g1

    if first == 0:
        for m in range(mb):
            s.db[m] = jnp.zeros((D, blk), F32)
    if lead:
        pre(first, 0, 0)

    def block(c, carry):
        for m in range(mb):
            if m + 1 < mb:
                pre(c, m + 1, (m + 1) % 2)
            else:
                pre(jnp.minimum(c + 1, limit - 1), 0, 0)
            mid(c, m, m % 2)
            if m > 0:
                post(c, m - 1, (m - 1) % 2)
            for at, call in hooks:
                if at == m:
                    call()
        post(c, mb - 1, (mb - 1) % 2)
        return carry

    lax.fori_loop(first, last, block, 0)


def norm_back(u, vhat, rs, gain):
    gu = u * gain
    return (gu - col_mean(gu) - vhat * col_mean(gu * vhat)) * rs


def add_to(s, which, first, value):
    s.acc[which] = value if first == 0 else s.acc[which] + value


def back_middle(s, m, blk):
    for at in range(0, blk, 128):
        cs = slice(at, at + 128)
        u = s.db[m, :, cs]
        vhat = s.vh2[m, :, cs]
        add_to(s, AG2, m + at, u * vhat)
        add_to(s, AC2, m + at, u)
        back = norm_back(u, vhat, s.rs2[m, 0:1, cs], s.col[OG2 : OG2 + D].astype(F32))
        dy = s.gt[m, :, cs].astype(F32) + back
        s.db[m, :, cs] = dy
        add_to(s, ABO, m + at, dy)
        s.zb[m % 2, D:, cs] = dy.astype(BF16)
    dp = s.zb[m % 2, D:, :]
    gwo = dot_t(s.ot[m], dp)
    s.ga[:, 3 * D :] = gwo if m == 0 else s.ga[:, 3 * D :] + gwo
    s.bt[m, 0:D, :] = dot_n(s.wo[...], dp).astype(BF16)


def back_attend(s, mb, blk, extra):
    half = blk // 2
    scale = HD ** (-0.5)

    def pre(i):
        m, part, head, qs, hr, pc = unit_of(i, blk)
        s.hs[i % 2, 0:half, 0:half] = dot_n(s.vn[m, qs, pc], pair_rows(s.bt[m, hr, qs], head))

    def mid(i):
        m, part, head, qs, hr, pc = unit_of(i, blk)
        for at in range(0, half, 128):
            cs = slice(at, at + 128)
            prob = s.prob[m, part, head, :, cs].astype(F32)
            weighted = prob * s.hs[i % 2, 0:half, cs]
            ds = weighted - prob * jnp.sum(weighted, axis=0, keepdims=True)
            s.zb[i % 2, 0:half, cs] = ds.astype(BF16)

    def post(i):
        m, part, head, qs, hr, pc = unit_of(i, blk)
        ds = s.zb[i % 2, 0:half, 0:half]
        dq = dot_n(s.kt[m, hr, qs], ds) * scale
        dk = dot_t(s.qt[m, hr, qs], ds)
        dv = dot_t(s.bt[m, hr, qs], s.prob[m, part, head])
        for c, value in enumerate((dq, dk, dv)):
            at = c * D + head * HD
            s.dqkv[m % 2, at : at + HD, qs] = value.astype(BF16)

    pipeline(mb * 2 * HEADS, pre, mid, post, extra)


def back_grads(s, m, blk):
    g = dot_t(s.at[m], s.dqkv[m % 2])
    s.ga[:, 0 : 3 * D] = g if m == 0 else s.ga[:, 0 : 3 * D] + g
    for at in range(0, blk, 128):
        cs = slice(at, at + 128)
        add_to(s, ABQ, m + at, s.dqkv[m % 2, 0:D, cs].astype(F32))
        add_to(s, ABV, m + at, s.dqkv[m % 2, 2 * D :, cs].astype(F32))


def back_rows(s, m, seg_ref, out_ref, dx_ref, blk):
    s.dz[m % 2, 0:D, :] = dot_n(s.wcat[...], s.dqkv[m % 2])
    for at in range(0, blk, 128):
        cs = slice(at, at + 128)
        u = s.dz[m % 2, 0:D, cs]
        vhat = s.vh1[m, :, cs]
        add_to(s, AG1, m + at, u * vhat)
        add_to(s, AC1, m + at, u)
        back = norm_back(u, vhat, s.rs1[m, 0:1, cs], s.col[OG1 : OG1 + D].astype(F32))
        s.dh[m % 2, D:, cs] = (s.db[m, :, cs] + back).astype(BF16)
        s.dh[m % 2, 0:D, cs] = s.out[m, :, cs].astype(BF16)
    start = start_of(seg_ref[m : m + 1, :])
    diff = iota((blk, blk), 0) - iota((blk, blk), 1)
    perm = one_hot((diff == start) | (diff == start - blk))
    both = dot_t(perm, s.dh[m % 2]).astype(BF16)
    out_ref[m * blk : (m + 1) * blk, :] = both[:, 0:D]
    dx_ref[m * blk : (m + 1) * blk, :] = both[:, D:]


def vector_row(s):
    ones = jnp.ones((16, 128), BF16)
    rows = []
    for which in range(8):
        v = s.acc[which]
        high = v.astype(BF16)
        low = (v - high.astype(F32)).astype(BF16)
        rows.append((dot_t(ones, high) + dot_t(ones, low))[0:8, :])
    return jnp.concatenate(rows + [s.g1[D : D + 8, :]], axis=1)


class Names:
    def __init__(self, keys, refs):
        for key, ref in zip(keys, refs):
            setattr(self, key, ref)


class Place:
    def __init__(self):
        wide = lax.axis_index("wide")
        narrow = lax.axis_index("narrow")
        self.z, self.y = lax.div(wide, 2), lax.rem(wide, 2)
        self.x, self.core = lax.div(narrow, 2), lax.rem(narrow, 2)

    def along(self, kind, k):
        if kind == "z":
            z = lax.rem(self.z + k, 4)
            return z, (z * 2 + self.y, self.x * 2 + self.core)
        x = self.x + (k % 2) * (1 - 2 * self.x)
        y = self.y + (k // 2) * (1 - 2 * self.y)
        return y * 2 + x, (self.z * 2 + y, x * 2 + self.core)

    def sibling(self):
        return (self.z * 2 + self.y, self.x * 2 + 1 - self.core)


def device_at(z, plane, core):
    return z * 8 + plane * 2 + core


def slot_of(device):
    return device % 2 * 16 + device // 2 % 4 * 4 + device // 8


def remote(src, dst, send, recv, device):
    return pltpu.make_async_remote_copy(
        src_ref=src, dst_ref=dst, send_sem=send, recv_sem=recv, device_id=device, device_id_type=MESH
    )


def greet(place):
    barrier = pltpu.get_barrier_semaphore()
    partners = [place.along(kind, k)[1] for kind in ("z", "plane") for k in (1, 2, 3)]
    partners.append(place.sibling())
    for partner in partners:
        pl.semaphore_signal(barrier, inc=1, device_id=partner, device_id_type=MESH)
    pl.semaphore_wait(barrier, len(partners))


class Gather:
    def __init__(self, place, buf, parts, send, recv):
        base = place.core * 16
        self.own = base + place.along("plane", 0)[0] * 4 + place.z
        n = len(parts)

        def copy(at, number, to):
            return remote(at, at, send.at[number], recv.at[number], to)

        def part_of(plane, part):
            first, count, lanes = part
            return buf.at[pl.ds(base + plane * 4 + first, count), :, lanes]

        self.first = [
            copy(buf.at[self.own], k - 1, place.along("z", k)[1]) for k in (1, 2, 3)
        ]
        self.second, self.third = [], []
        for p, part in enumerate(parts):
            mine = part_of(place.along("plane", 0)[0], part)
            self.second.append(
                [copy(mine, 2 + 3 * p + k, place.along("plane", k)[1]) for k in (1, 2, 3)]
            )
            self.third.append(
                [
                    copy(
                        part_of(place.along("plane", k)[0], part),
                        3 + 3 * n + 4 * p + k,
                        place.sibling(),
                    )
                    for k in range(4)
                ]
            )

    def start_first(self):
        for copy in self.first:
            copy.start()

    def arrive_first(self):
        for copy in self.first:
            copy.wait_recv()

    def start_second(self, part):
        for copy in self.second[part]:
            copy.start()
        self.third[part][0].start()

    def start_third(self, part):
        for copy, after in zip(self.second[part], self.third[part][1:]):
            copy.wait_recv()
            after.start()

    def finish(self, part):
        for copy in self.third[part]:
            copy.wait_recv()

    def close(self):
        for copy in sum(self.second + self.third, self.first):
            copy.wait_send()


class FastGather:
    def __init__(self, place, buf, send, recv):
        base = place.core * 16
        group = base + place.along("plane", 0)[0] * 4
        self.own = group + place.z

        def copy(at, number, to):
            return remote(at, at, send.at[number], recv.at[number], to)

        self.first = [
            copy(buf.at[self.own], k - 1, place.along("z", k)[1]) for k in (1, 2, 3)
        ]
        self.second = []
        for k in range(4):
            at = buf.at[group + place.along("z", (4 - k) % 4)[0]]
            self.second.append(
                [copy(at, 2 + 3 * k + j, place.along("plane", j)[1]) for j in (1, 2, 3)]
            )
        self.third = [
            copy(
                buf.at[pl.ds(base + place.along("plane", k)[0] * 4, 4)], 15 + k, place.sibling()
            )
            for k in range(4)
        ]

    def start_first(self):
        for copy in self.first + self.second[0]:
            copy.start()

    def start_second(self):
        for k in (1, 2, 3):
            self.first[k - 1].wait_recv()
            for copy in self.second[k]:
                copy.start()
        self.third[0].start()

    def start_third(self):
        for j in (1, 2, 3):
            for k in range(4):
                self.second[k][j - 1].wait_recv()
            self.third[j].start()

    def finish(self):
        for copy in self.third:
            copy.wait_recv()
        for copy in sum(self.second, self.first) + self.third:
            copy.wait_send()


class Scatter:
    def __init__(self, place, line, own, done, buf, got, held, send, recv):
        self.place, self.line, self.own, self.done = place, line, own, done
        self.buf, self.got, self.held = buf, got, held
        n = len(line)
        self.first, self.second, self.third = [], [], []
        for k in range(4):
            at = pl.ds(place.along("plane", k)[0] * n, n)
            self.first.append(
                remote(buf.at[at], got.at[at], send.at[k], recv.at[k], place.sibling())
            )
        for k in (1, 2, 3):
            at = pl.ds((3 + k) * n, n)
            to = place.along("plane", k)[1]
            self.second.append(
                remote(buf.at[at], got.at[at], send.at[3 + k], recv.at[3 + k], to)
            )
            at = 7 * n + k - 1
            to = place.along("z", k)[1]
            self.third.append(
                remote(buf.at[at], got.at[at], send.at[6 + k], recv.at[6 + k], to)
            )

    def owned(self, z, call):
        if len(self.line) == 4:
            call()
        else:
            pl.when((z >= self.line[0]) & (z <= self.line[-1]))(call)

    def start_first(self):
        n = len(self.line)
        for plane in range(4):
            for j, z in enumerate(self.line):
                term = self.own(device_at(z, plane, 1 - self.place.core))
                self.buf[plane * n + j] = term.astype(BF16)
        for k in (3, 1, 2, 0):
            self.first[k].start()

    def start_second(self):
        n = len(self.line)
        for k in (3, 1, 2, 0):
            self.first[k].wait_recv()
            plane = self.place.along("plane", k)[0]
            for j, z in enumerate(self.line):
                term = self.own(device_at(z, plane, self.place.core))
                term = term + self.got[plane * n + j].astype(F32)
                if k == 0:
                    self.held[j] = term
                else:
                    self.buf[(3 + k) * n + j] = term.astype(BF16)
            if k > 0:
                self.second[k - 1].start()

    def start_third(self):
        n = len(self.line)
        for copy in self.second:
            copy.wait_recv()
        for j in range(n):
            term = self.held[j]
            for k in (1, 2, 3):
                term = term + self.got[(3 + k) * n + j].astype(F32)
            self.held[j] = term
        for k in (1, 2, 3):
            z = self.place.along("z", k)[0]

            def send(k=k, z=z):
                self.buf[7 * n + k - 1] = self.held[z - self.line[0]].astype(BF16)
                self.third[k - 1].start()

            self.owned(z, send)

    def finish(self):
        n = len(self.line)

        def take():
            term = self.held[self.place.z - self.line[0]]
            for k in (1, 2, 3):
                self.third[k - 1].wait_recv()
                term = term + self.got[7 * n + k - 1].astype(F32)
            self.done(term)

        self.owned(self.place.z, take)
        for copy in self.first + self.second:
            copy.wait_send()
        for k in (1, 2, 3):
            self.owned(self.place.along("z", k)[0], self.third[k - 1].wait_send)


def entry_place(k):
    gain, rest = k < 512.0, k - 512.0
    device = jnp.where(gain, jnp.floor((k + 0.5) * (1.0 / 16)), jnp.floor((rest + 0.5) * (1.0 / 112)))
    lane = jnp.where(gain, k - 16.0 * device, rest - 112.0 * device + 16.0)
    return device, lane


def pick_at(s, at):
    ref = s.w1t if at < FF else s.w2
    return ref.at[at % FF : at % FF + 512]


def make_tables(s):
    row = iota((8, 256), 1)
    slot = row // 8
    device = slot % 4 * 8 + slot // 4 % 4 * 2 + slot // 16
    first_gain = jnp.where(row % 8 == 0, 16 * device, 8192)[0:1, :]
    first_bias = jnp.where(row % 8 == 0, 512 + 112 * device, 8192)[0:1, :]
    for at in range(0, NVEC, 512):
        k = iota((512, 256), 0) + at
        first, count = (first_gain, 16) if at < 512 else (first_bias, 112)
        pick_at(s, at)[...] = one_hot((k >= first) & (k < first + count))
        _, lane = entry_place((iota((512, 128), 0) + at).astype(F32))
        s.keep[at : at + 512, :] = one_hot(lane == iota((512, 128), 1).astype(F32))
    device, _ = entry_place(iota((16, NVEC), 1).astype(F32))
    for at in (0, 16):
        s.mine[at : at + 16, :] = one_hot(device == (iota((16, NVEC), 0) + at).astype(F32))


def unpack_attention(s):
    for c in range(4):
        rows = [s.bufa[slot_of(d), 8 * c : 8 * c + 8, :].astype(F32) for d in range(32)]
        full = jnp.concatenate(rows, axis=0).astype(BF16)
        if c < 3:
            s.wcat[:, c * D : (c + 1) * D] = full
        else:
            s.wo[...] = full
    rows = [s.bufa[d, 32:40, 0:128].astype(F32) for d in range(32)]
    table = jnp.concatenate(rows, axis=0).astype(BF16)
    ones = jnp.ones((128, 128), BF16)
    for at in range(0, NVEC, 512):
        found = dot_n(pick_at(s, at)[...], table).astype(BF16) * s.keep[at : at + 512, :]
        s.col[at : at + 512, :] = dot_n(found, ones).astype(BF16)


def unpack_inner(s, half):
    for i in range(16):
        pair = [
            s.buf1[slot_of(2 * i + c), :, half * 512 : half * 512 + 512].astype(F32) for c in range(2)
        ]
        for h in range(2):
            rows = jnp.concatenate([v[8 * h : 8 * h + 8] for v in pair], axis=0)
            at = half * (FF // 2) + h * (FF // 4)
            s.w1[16 * i : 16 * i + 16, at : at + FF // 4] = rows.astype(BF16)
    for d in range(16 * half, 16 * half + 16):
        s.w2[64 * d : 64 * d + 64, :] = s.buf2[slot_of(d)]


def vector_rows(s):
    row = vector_row(s)[0:1, :]
    high = row.astype(BF16).astype(F32)
    total = None
    for term in (high, row - high):
        part = dot_n((s.mine[...].astype(F32) * term).astype(BF16), s.keep[...])
        total = part if total is None else total + part
    high = total.astype(BF16).astype(F32)
    s.vrow[:, 0:128] = high
    s.vrow[:, 128:256] = total - high


def fold(rows):
    half = rows.shape[1] // 2
    return jnp.concatenate([rows[:, :half], rows[:, half:]], axis=0)


def own_attention(s, cols):
    return lambda device: fold(s.ga[pl.ds(pl.multiple_of(device * 8, 8), 8), cols])


def own_vector(s):
    return lambda device: fold(jnp.broadcast_to(s.vrow[pl.ds(device, 1), :], (8, D)))


def own_first(s, half):
    cols = slice(half * (FF // 2), (half + 1) * (FF // 2))
    return lambda device: fold(s.g1[pl.ds(pl.multiple_of(device * 8, 8), 8), cols])


def own_second(s):
    return lambda device: s.g2[pl.ds(pl.multiple_of(device * 64, 64), 64), :]


MSG = 40
SUMS = {
    "q": (4, 16, 3 * D // 2),
    "o": (4, 16, D // 2),
    "v": (4, 16, D // 2),
    "1x": (4, 16, FF // 4),
    "1y": (4, 16, FF // 4),
    "2x": (2, 64, D),
    "2y": (2, 64, D),
}


def fused_scratch(mb, blk):
    shapes = scratch_shapes(mb, blk)
    for name, (rows, cols) in (("a", (MSG, D)), ("1", (16, FF // 2)), ("2", (64, D))):
        shapes["buf" + name] = pltpu.VMEM((32, rows, cols), BF16)
        shapes["gsend" + name] = pltpu.SemaphoreType.DMA((19,))
        shapes["grecv" + name] = pltpu.SemaphoreType.DMA((19,))
    for name, (n, rows, cols) in SUMS.items():
        if name != "2x":
            shapes["out" + name] = pltpu.VMEM((7 * n + 3, rows, cols), BF16)
        shapes["got" + name] = pltpu.VMEM((7 * n + 3, rows, cols), BF16)
        shapes["held" + name] = pltpu.VMEM((n, rows, cols), F32)
        shapes["ssend" + name] = pltpu.SemaphoreType.DMA((10,))
        shapes["srecv" + name] = pltpu.SemaphoreType.DMA((10,))
    shapes["keep"] = pltpu.VMEM((NVEC, 128), BF16)
    shapes["mine"] = pltpu.VMEM((32, NVEC), BF16)
    shapes["vrow"] = pltpu.VMEM((32, D), F32)
    shapes["line"] = pltpu.VMEM((8, D), F32)
    for name in ("xs", "gs"):
        shapes[name] = pltpu.VMEM((mb * blk, D), BF16)
    shapes["insem"] = pltpu.SemaphoreType.DMA((2,))
    shapes["outsem"] = pltpu.SemaphoreType.DMA((2 * mb,))
    return shapes


def fused_kernel(keys, mb, blk, *refs):
    x_hbm, seg_ref, g_hbm, wa, w1, w2, gains, biases = refs[:8]
    out_hbm, dx_hbm, sumq, sumo, sumv, sum1, sum2 = refs[8:15]
    s = Names(keys, refs[15:])
    place = Place()
    loads = []
    for i, (hbm, ref) in enumerate(((x_hbm, s.xs), (g_hbm, s.gs))):
        loads.append(pltpu.make_async_copy(hbm, ref, s.insem.at[i]))
        loads[-1].start()
    refs = {n: [getattr(s, key + n) for key in ("buf", "gsend", "grecv")] for n in "a12"}
    every = slice(None)
    gather = {
        "a": FastGather(place, *refs["a"]),
        "1": Gather(
            place,
            refs["1"][0],
            [(0, 4, slice(0, FF // 4)), (0, 4, slice(FF // 4, FF // 2))],
            *refs["1"][1:],
        ),
        "2": Gather(place, refs["2"][0], [(0, 2, every), (2, 2, every)], *refs["2"][1:]),
    }
    s.line[...] = jnp.zeros((8, D), F32)
    s.line[0:1, 0:16] = gains[...]
    s.line[0:1, 16:128] = biases[...]
    own = jnp.concatenate([wa[c] for c in range(4)] + [s.line[...]], axis=0).astype(BF16)
    s.bufa[gather["a"].own] = own
    first = jnp.concatenate([fold(w1[:, 0 : FF // 2]), fold(w1[:, FF // 2 :])], axis=1)
    s.buf1[gather["1"].own] = first.astype(BF16)
    s.buf2[gather["2"].own] = w2[...].astype(BF16)
    greet(place)
    gather["a"].start_first()
    gather["1"].start_first()
    gather["2"].start_first()
    make_tables(s)
    gather["a"].start_second()
    for copy in loads:
        copy.wait()
    for m in range(mb):
        load_rows(s, m, s.xs, s.gs, seg_ref, blk)
    gather["a"].start_third()
    for n in "12":
        gather[n].arrive_first()
    for part in range(2):
        for n in "12":
            gather[n].start_second(part)
    gather["a"].finish()
    unpack_attention(s)
    transpose_weights_attention(s)
    project(s, 0, blk)
    project(s, 1, blk)
    extra = {}

    def at(step, f, *args):
        extra.setdefault(step, []).append(functools.partial(f, *args))

    for m in range(mb):
        if m + 2 < mb:
            at(8 * m + 4, project, s, m + 2, blk)
        at(8 * m + 8, middle, s, m, blk)
    for n in "12":
        at(22, gather[n].start_third, 0)
    attend(s, mb, blk, extra)
    for n in "12":
        gather[n].finish(0)
    unpack_inner(s, 0)
    transpose_weights_inner(s, range(4))
    scatter = {}
    s.out2x = s.buf2.at[0:17]

    def sum_into(name, line, own, done):
        refs = [getattr(s, key + name) for key in ("out", "got", "held", "ssend", "srecv")]
        scatter[name] = Scatter(place, line, own, done, *refs)

    def into(ref):
        def store(value):
            ref[...] = value

        return store

    def into_first(half):
        def store(value):
            for part in range(2):
                at = (2 * half + part) * FF // 4
                sum1[:, at : at + FF // 4] = value[8 * part : 8 * part + 8]

        return store

    sum_into("q", range(4), own_attention(s, slice(0, 3 * D)), into(sumq))
    sum_into("o", range(4), own_attention(s, slice(3 * D, 4 * D)), into(sumo))
    sum_into("v", range(4), own_vector(s), into(sumv))
    for half, name in enumerate("xy"):
        sum_into("1" + name, range(4), own_first(s, half), into_first(half))
        sum_into("2" + name, range(2 * half, 2 * half + 2), own_second(s), into(sum2))
    feed_forward(s, mb, blk, first=0, last=1, limit=2)
    for n in "12":
        gather[n].start_third(1)
    feed_forward(s, mb, blk, first=1, last=2, lead=False, limit=2)
    for n in "12":
        gather[n].finish(1)
        gather[n].close()
    unpack_inner(s, 1)
    transpose_weights_inner(s, range(4, 8))
    scatter["1x"].start_first()
    scatter["2x"].start_first()
    later = [(2, scatter[n].start_second) for n in ("1x", "2x")]
    feed_forward(s, mb, blk, first=2, last=3, hooks=later)
    feed_forward(s, mb, blk, first=3, last=4, lead=False)
    scatter["1y"].start_first()
    scatter["2y"].start_first()
    saves = []

    def last_rows(m):
        back_rows(s, m, seg_ref, s.xs, s.gs, blk)
        rows = pl.ds(m * blk, blk)
        for kind, (ref, hbm) in enumerate(((s.xs, out_hbm), (s.gs, dx_hbm))):
            sem = s.outsem.at[2 * m + kind]
            saves.append(pltpu.make_async_copy(ref.at[rows], hbm.at[rows], sem))
            saves[-1].start()

    back_middle(s, 0, blk)
    extra.clear()
    for m in range(mb):
        if m + 1 < mb:
            at(8 * m + 3, back_middle, s, m + 1, blk)
        at(8 * m + 8, back_grads, s, m, blk)
        if m + 2 < mb:
            at(8 * m + 9, last_rows, m)
    for n in "12":
        at(3, scatter[n + "x"].start_third)
        at(6, scatter[n + "y"].start_second)
        at(24, scatter[n + "x"].finish)
        at(30, scatter[n + "y"].start_third)
    at(22, scatter["o"].start_first)
    at(27, scatter["o"].start_second)
    back_attend(s, mb, blk, extra)
    scatter["q"].start_first()
    last_rows(mb - 2)
    scatter["q"].start_second()
    last_rows(mb - 1)
    vector_rows(s)
    scatter["v"].start_first()
    scatter["o"].start_third()
    scatter["v"].start_second()
    scatter["1y"].finish()
    scatter["2y"].finish()
    scatter["q"].start_third()
    scatter["v"].start_third()
    scatter["o"].finish()
    for copy in saves:
        copy.wait()
    scatter["q"].finish()
    scatter["v"].finish()


STEP = 10
BETA_ONE = 0.9
BETA_TWO = 0.999
ADAM_EPS = 1e-08
RATES = (0.08, 0.08, 0.08, 0.6, 0.6)
DECAYS = (0.01, 0.01, 0.01, 0.0, 0.0)


def adamw(weight, grad, first, second, rate, decay):
    first_new = BETA_ONE * first + (1.0 - BETA_ONE) * grad
    second_new = BETA_TWO * second + (1.0 - BETA_TWO) * grad * grad
    first_hat = first_new / (1.0 - BETA_ONE**STEP)
    second_hat = second_new / (1.0 - BETA_TWO**STEP)
    weight_new = weight - rate * (first_hat / (jnp.sqrt(second_hat) + ADAM_EPS) + decay * weight)
    return weight_new, first_new, second_new


def adam_kernel(*refs):
    sumq, sumo, sumv, sum1, sum2 = refs[:5]
    state, rows, new, saved, sem = refs[5:20], refs[20:22], refs[22:37], refs[37:39], refs[39]
    copies = [pltpu.make_async_copy(rows[i], saved[i], sem.at[i]) for i in range(2)]
    for copy in copies:
        copy.start()

    def update(member, grad, at=()):
        at = at if at else (slice(None),)
        values = adamw(
            state[member][at], grad, state[5 + member][at], state[10 + member][at], RATES[member], DECAYS[member]
        )
        for kind in range(3):
            new[5 * kind + member][at] = values[kind]

    grads = jnp.concatenate([sumq[0:8, :], sumq[8:16, :], sumo[0:8, :], sumo[8:16, :]], axis=1)
    for c in range(4):
        update(0, grads[:, c * D : (c + 1) * D], (c,))
    update(1, sum1[...])
    update(2, sum2[...])
    line = sumv[0:1, :] + sumv[8:9, :]
    update(3, line[:, 0:16])
    update(4, line[:, 16:128])
    for copy in copies:
        copy.wait()


VMEM_SPEC = pl.BlockSpec(memory_space=pltpu.VMEM)
ANY_SPEC = pl.BlockSpec(memory_space=pl.ANY)


def fused_device(*args):
    frames, segments, out_grad = args[:3]
    rows = lambda v: v.reshape(1, -1) if v.ndim == 1 else v
    state = [rows(v) for v in args[3:]]
    mb, blk = segments.shape
    shapes = fused_scratch(mb, blk)
    like = lambda v: jax.ShapeDtypeStruct(v.shape, v.dtype)
    out, dx, *sums = pl.pallas_call(
        functools.partial(fused_kernel, list(shapes), mb, blk),
        out_shape=[like(frames), like(frames)]
        + [jax.ShapeDtypeStruct(t, F32) for t in ((16, 3 * D // 2), (16, D // 2), (16, D // 2), (8, FF), (64, D))],
        in_specs=[ANY_SPEC, VMEM_SPEC, ANY_SPEC] + [VMEM_SPEC] * 5,
        out_specs=[ANY_SPEC] * 2 + [VMEM_SPEC] * 5,
        scratch_shapes=list(shapes.values()),
        compiler_params=pltpu.CompilerParams(
            collective_id=0, has_side_effects=True, vmem_limit_bytes=63 * 2**20
        ),
    )(frames, segments, out_grad, *state[:5])
    *new, out, dx = pl.pallas_call(
        adam_kernel,
        out_shape=[like(v) for v in state] + [like(out), like(dx)],
        in_specs=[VMEM_SPEC] * 22,
        out_specs=[VMEM_SPEC] * 15 + [ANY_SPEC] * 2,
        scratch_shapes=[pltpu.SemaphoreType.DMA((2,))],
    )(*sums, *state, out, dx)
    return (out, dx, *[v.reshape(t.shape) for v, t in zip(new, args[3:])])


def local_kernel(keys, mb, blk, *refs):
    x_ref, seg_ref, g_ref, wa, w1, w2, col = refs[:7]
    out_ref, dx_ref, ga, g1, g2, gv = refs[7:13]
    s = Names(keys, refs[13:])
    for c in range(3):
        s.wcat[:, c * D : (c + 1) * D] = wa[c]
    s.wo[...] = wa[3]
    s.w1[...] = w1[...]
    s.w2[...] = w2[...]
    s.col[...] = col[...].astype(BF16)
    transpose_weights_attention(s)
    transpose_weights_inner(s, range(FF // D))
    for m in range(mb):
        load_rows(s, m, x_ref, g_ref, seg_ref, blk)
        project(s, m, blk)
    attend(s, mb, blk, {})
    for m in range(mb):
        middle(s, m, blk)
    feed_forward(s, mb, blk)
    extra = {}
    for m in range(mb):
        back_middle(s, m, blk)
        extra[8 * m + 8] = [
            functools.partial(back_grads, s, m, blk),
            functools.partial(back_rows, s, m, seg_ref, out_ref, dx_ref, blk),
        ]
    back_attend(s, mb, blk, extra)
    gv[...] = vector_row(s)
    ga[...] = s.ga[...]
    g1[...] = s.g1[0:D, :]
    g2[...] = s.g2[...]


AXES = ("wide", "narrow")


def local_device(*args):
    frames, segments, out_grad = args[:3]
    weights, firsts, seconds = args[3:8], args[8:13], args[13:18]
    dims = (1, 0, 0, 0, 0)
    full = [
        lax.all_gather(w.astype(BF16), AXES, axis=dim, tiled=True) for w, dim in zip(weights, dims)
    ]
    mb, blk = segments.shape
    table = jnp.concatenate([full[3], full[4]]).astype(F32)
    shapes = scratch_shapes(mb, blk)
    like = lambda v: jax.ShapeDtypeStruct(v.shape, v.dtype)
    out, dx, ga, g1, g2, gv = pl.pallas_call(
        functools.partial(local_kernel, list(shapes), mb, blk),
        out_shape=[like(frames), like(frames)]
        + [jax.ShapeDtypeStruct(t, F32) for t in ((D, 4 * D), (D, FF), (FF, D), (8, NVEC))],
        in_specs=[VMEM_SPEC] * 7,
        out_specs=[VMEM_SPEC] * 6,
        scratch_shapes=list(shapes.values()),
        compiler_params=pltpu.CompilerParams(vmem_limit_bytes=63 * 2**20),
    )(frames, segments, out_grad, *full[:3], jnp.broadcast_to(table[:, None], (NVEC, 128)))
    grads = (jnp.stack(jnp.split(ga, 4, axis=1)), g1, g2, gv[0, :512], gv[0, 512:])
    owned = [
        lax.psum_scatter(g, AXES, scatter_dimension=dim, tiled=True) for g, dim in zip(grads, dims)
    ]
    new = [adamw(*v) for v in zip(weights, owned, firsts, seconds, RATES, DECAYS)]
    return (out, dx, *[new[member][kind] for kind in range(3) for member in range(5)])


def solution(mesh):
    rows, matrix, vector = P(AXES, None), P(None, AXES, None), P(AXES)
    group = (matrix, rows, rows, vector, vector)
    fits = (mesh.shape["wide"], mesh.shape["narrow"]) == (8, 4)
    return jax.shard_map(
        fused_device if fits else local_device,
        mesh=mesh,
        in_specs=(rows, rows, rows, *group, *group, *group),
        out_specs=(rows, rows, *group, *group, *group),
        check_vma=False,
    )
```

```python
import functools
import jax
import jax.numpy as jnp
from jax import lax
from jax.experimental import pallas as pl
from jax.experimental.pallas import tpu as pltpu
from jax.sharding import PartitionSpec as P

D = 256
HEADS = 4
HD = 64
FF = 2048
NORM_EPS = 1e-05
C_ONE = 0.7978845608028654
C_THREE = C_ONE * 0.044715
F32 = jnp.float32
BF16 = jnp.bfloat16


MESH = pl.DeviceIdType.MESH


def dot_n(a, b):
    return jnp.dot(a, b, preferred_element_type=F32)


def dot_t(a, b):
    return lax.dot_general(a, b, (((1,), (1,)), ((), ())), preferred_element_type=F32)


def iota(shape, dim):
    return lax.broadcasted_iota(jnp.int32, shape, dim)


def one_hot(cond):
    return jnp.where(cond, 1.0, 0.0).astype(BF16)


def eye():
    return one_hot(iota((D, D), 0) == iota((D, D), 1))


def wide_of(col, width):
    return jnp.concatenate([col] * (width // 128), axis=1)


def lane_fold(v):
    total = v[:, 0:128]
    for at in range(128, v.shape[1], 128):
        total = total + v[:, at : at + 128]
    return total


def col_mean(v):
    return jnp.sum(v, axis=0, keepdims=True) * (1.0 / v.shape[0])


def start_of(seg):
    start = jnp.full((1, 1), 4096.0, F32)
    for v in range(4):
        count = jnp.sum(jnp.where(seg == v, 1.0, 0.0), axis=1, keepdims=True)
        below = jnp.sum(jnp.where(seg < v, 1.0, 0.0), axis=1, keepdims=True)
        start = jnp.minimum(start, jnp.where(count == 256.0, below, 4096.0))
    return start.astype(jnp.int32)


def gelu_both(h):
    h2 = h * h
    t = jnp.tanh(h * (C_THREE * h2 + C_ONE))
    s = 0.5 * t + 0.5
    z = h * s
    slope = s + z * (1.0 - s) * (6.0 * C_THREE * h2 + 2.0 * C_ONE)
    return z, slope


OG1, OG2, OBQ, OBV, OBO, OB2, OC1, OC2, OB1 = 0, 256, 512, 768, 1024, 1280, 1536, 1792, 2048
NVEC = 4096
AG1, AG2, ABQ, ABV, ABO, AB2, AC1, AC2 = range(8)


def scratch_shapes(mb, blk):
    half = blk // 2
    return dict(
        wqkvt=pltpu.VMEM((3 * D, D), BF16),
        wcat=pltpu.VMEM((D, 3 * D), BF16),
        wo=pltpu.VMEM((D, D), BF16),
        wot=pltpu.VMEM((D, D), BF16),
        w1=pltpu.VMEM((D, FF), BF16),
        w1t=pltpu.VMEM((FF, D), BF16),
        w2=pltpu.VMEM((FF, D), BF16),
        w2t=pltpu.VMEM((D, FF), BF16),
        col=pltpu.VMEM((NVEC, 128), BF16),
        vh1=pltpu.VMEM((mb, D, blk), F32),
        rs1=pltpu.VMEM((mb, 8, blk), F32),
        bias=pltpu.VMEM((mb, half, half), BF16),
        vh2=pltpu.VMEM((mb, D, blk), F32),
        rs2=pltpu.VMEM((mb, 8, blk), F32),
        at=pltpu.VMEM((mb, D, blk), BF16),
        bt=pltpu.VMEM((mb, D + 16, blk), BF16),
        gt=pltpu.VMEM((mb, D, blk), BF16),
        qt=pltpu.VMEM((mb, D, blk), BF16),
        kt=pltpu.VMEM((mb, D, blk), BF16),
        vt=pltpu.VMEM((mb, D, blk), BF16),
        vn=pltpu.VMEM((mb, blk, D), BF16),
        ot=pltpu.VMEM((mb, D, blk), BF16),
        prob=pltpu.VMEM((mb, 2, HEADS, half, half), BF16),
        out=pltpu.VMEM((mb, D, blk), F32),
        db=pltpu.VMEM((mb, D, blk), F32),
        hs=pltpu.VMEM((2, 512, blk), F32),
        dz=pltpu.VMEM((2, 512, blk), F32),
        zb=pltpu.VMEM((2, 512, blk), BF16),
        dh=pltpu.VMEM((2, 512, blk), BF16),
        dqkv=pltpu.VMEM((2, 3 * D, blk), BF16),
        acc=pltpu.VMEM((8, D, 128), F32),
        g1=pltpu.VMEM((D + 16, FF), F32),
        g2=pltpu.VMEM((FF, D), F32),
        ga=pltpu.VMEM((D, 4 * D), F32),
    )


def transpose_weights_attention(s):
    unit = eye()
    for c in range(3):
        s.wqkvt[c * D : (c + 1) * D, :] = dot_t(unit, s.wcat[:, c * D : (c + 1) * D]).astype(BF16)
    s.wot[...] = dot_t(unit, s.wo[...]).astype(BF16)


def transpose_weights_inner(s, blocks):
    unit = eye()
    for c in blocks:
        cs = slice(c * D, (c + 1) * D)
        s.w1t[cs, :] = dot_t(unit, s.w1[:, cs]).astype(BF16)
        s.w2t[:, cs] = dot_t(unit, s.w2[cs, :]).astype(BF16)


def col_of(s, at, width):
    return wide_of(s.col[at : at + D, :].astype(F32), width)


def norm_of(v):
    center = v - col_mean(v)
    rs = lax.rsqrt(col_mean(center * center) + NORM_EPS)
    return center * rs, rs


def load_rows(s, m, x_ref, g_ref, seg_ref, blk):
    start = start_of(seg_ref[m : m + 1, :])
    rows = slice(m * blk, (m + 1) * blk)
    diff = iota((blk, blk), 1) - iota((blk, blk), 0)
    perm = one_hot((diff == start) | (diff == start - blk))
    both = jnp.concatenate([x_ref[rows, :], g_ref[rows, :]], axis=1)
    rolled = dot_n(perm, both).astype(BF16)
    unit = eye()
    s.out[m] = dot_t(unit, rolled[:, 0:D])
    s.gt[m] = dot_t(unit, rolled[:, D : 2 * D]).astype(BF16)
    for at in range(0, blk, 128):
        cs = slice(at, at + 128)
        vhat, rs = norm_of(s.out[m, :, cs])
        s.vh1[m, :, cs] = vhat
        s.rs1[m, :, cs] = jnp.broadcast_to(rs, (8, 128))
        add_to(s, AB2, m + at, s.gt[m, :, cs].astype(F32))
    seg = seg_ref[m : m + 1, :].astype(F32).astype(BF16)
    tail = perm[blk // 2 :, :]
    seg_row = dot_t(jnp.broadcast_to(seg, (16, blk)), tail)[0:1, :]
    seg_col = dot_t(tail, jnp.broadcast_to(seg, (128, blk)))
    bias = jnp.where(wide_of(seg_col, blk // 2) == seg_row, 0.0, -1e30)
    s.bias[m] = bias.astype(BF16)


def project(s, m, blk):
    for at in range(0, blk, 128):
        cs = slice(at, at + 128)
        a = s.vh1[m, :, cs] * s.col[OG1 : OG1 + D].astype(F32) + s.col[OC1 : OC1 + D].astype(F32)
        s.at[m, :, cs] = a.astype(BF16)
    qkv = dot_n(s.wqkvt[...], s.at[m])
    q = (qkv[0:D] + col_of(s, OBQ, blk)).astype(BF16)
    s.qt[m] = q * jnp.asarray(HD ** (-0.5), BF16)
    k = qkv[D : 2 * D].astype(BF16)
    v = (qkv[2 * D :] + col_of(s, OBV, blk)).astype(BF16)
    s.kt[m] = k
    s.vt[m] = v
    unit = eye()
    for at in range(0, blk, D):
        s.dqkv[m % 2, at : at + D, m // 2 * D : m // 2 * D + D] = dot_t(unit, k[:, at : at + D]).astype(BF16)
        s.vn[m, at : at + D, :] = dot_t(unit, v[:, at : at + D]).astype(BF16)


PAIRS = HEADS // 2


def unit_of(i, blk):
    half = blk // 2
    m, part, pair = i // (2 * PAIRS), i // PAIRS % 2, i % PAIRS
    return m, part, pair, slice(part * half, (part + 1) * half), slice(pair * 128, pair * 128 + 128)


def pair_blocks(v):
    zero = jnp.zeros_like(v[0:HD])
    top = jnp.concatenate([v[0:HD], zero], axis=1)
    return jnp.concatenate([top, jnp.concatenate([zero, v[HD:]], axis=1)], axis=0)


def pipeline(units, pre, mid, post, extra):
    for i in range(-1, units + 1):
        if i + 1 < units:
            pre(i + 1)
        if 0 <= i < units:
            mid(i)
        if i >= 1:
            post(i - 1)
        for call in extra.get(i, ()):
            call()


def attend(s, mb, blk, extra):
    half = blk // 2

    def pre(i):
        m, part, pair, qs, pc = unit_of(i, blk)
        keys = s.dqkv[m % 2, qs, m // 2 * D + pc.start : m // 2 * D + pc.stop]
        s.hs[i % 2, 0:half, :] = dot_n(keys, pair_blocks(s.qt[m, pc, qs]))

    def mid(i):
        m, part, pair, qs, pc = unit_of(i, blk)
        for at in range(0, blk, 128):
            head, cs = at // half, slice(at % half, at % half + 128)
            st = s.hs[i % 2, 0:half, at : at + 128]
            if part == 1:
                st = st + s.bias[m, :, cs].astype(F32)
            e = jnp.exp(st - jnp.max(st, axis=0, keepdims=True))
            prob = e * (1.0 / jnp.sum(e, axis=0, keepdims=True))
            s.prob[m, part, 2 * pair + head, :, cs] = prob.astype(BF16)

    def post(i):
        m, part, pair, qs, pc = unit_of(i, blk)
        for head in range(2):
            hr = slice(pc.start + head * HD, pc.start + head * HD + HD)
            mixed = dot_n(s.vt[m, hr, qs], s.prob[m, part, 2 * pair + head])
            s.ot[m, hr, qs] = mixed.astype(BF16)

    pipeline(mb * 2 * PAIRS, pre, mid, post, extra)


def middle(s, m, blk):
    s.dz[m % 2, 0:D, :] = dot_n(s.wot[...], s.ot[m])
    s.bt[m, D:, :] = jnp.ones((16, blk), BF16)
    for at in range(0, blk, 128):
        cs = slice(at, at + 128)
        y = s.out[m, :, cs] + s.dz[m % 2, 0:D, cs] + s.col[OBO : OBO + D].astype(F32)
        vhat, rs = norm_of(y)
        s.vh2[m, :, cs] = vhat
        s.rs2[m, :, cs] = jnp.broadcast_to(rs, (8, 128))
        s.bt[m, 0:D, cs] = (vhat * s.col[OG2 : OG2 + D].astype(F32) + s.col[OC2 : OC2 + D].astype(F32)).astype(BF16)
        s.out[m, :, cs] = y + s.col[OB2 : OB2 + D].astype(F32)


def feed_forward(s, mb, blk, fc=512, br=32, first=0, last=FF // 512, lead=True, limit=FF // 512, hooks=()):
    def pre(c, m, p):
        cs = pl.ds(pl.multiple_of(c * fc, fc), fc)
        s.hs[p] = dot_n(s.w1t[cs, :], s.bt[m, 0:D, :])
        s.dz[p] = dot_n(s.w2[cs, :], s.gt[m])

    def mid(c, m, p):
        for r in range(0, fc, br):
            rs = slice(r, r + br)
            bias = s.col[pl.ds(pl.multiple_of(OB1 + c * fc + r, br), br), :].astype(F32)
            z, slope = gelu_both(s.hs[p, rs, :] + wide_of(bias, blk))
            s.zb[p, rs, :] = z.astype(BF16)
            s.dh[p, rs, :] = (s.dz[p, rs, :] * slope).astype(BF16)

    def post(c, m, p):
        cs = pl.ds(pl.multiple_of(c * fc, fc), fc)
        z, dh = s.zb[p], s.dh[p]
        s.out[m] = s.out[m] + dot_n(s.w2t[:, cs], z)
        d = dot_n(s.w1[:, cs], dh)
        s.db[m] = s.db[m] + d
        g2 = dot_t(z, s.gt[m])
        g1 = dot_t(s.bt[m], dh)
        s.g2[cs, :] = g2 if m == 0 else s.g2[cs, :] + g2
        s.g1[:, cs] = g1 if m == 0 else s.g1[:, cs] + g1

    if first == 0:
        for m in range(mb):
            s.db[m] = jnp.zeros((D, blk), F32)
    if lead:
        pre(first, 0, 0)

    def block(c, carry):
        for m in range(mb):
            if m + 1 < mb:
                pre(c, m + 1, (m + 1) % 2)
            else:
                pre(jnp.minimum(c + 1, limit - 1), 0, 0)
            mid(c, m, m % 2)
            if m > 0:
                post(c, m - 1, (m - 1) % 2)
            for at, call in hooks:
                if at == m:
                    call()
        post(c, mb - 1, (mb - 1) % 2)
        return carry

    lax.fori_loop(first, last, block, 0)


def norm_back(u, vhat, rs, gain):
    gu = u * gain
    return (gu - col_mean(gu) - vhat * col_mean(gu * vhat)) * rs


def add_to(s, which, first, value):
    s.acc[which] = value if first == 0 else s.acc[which] + value


def back_middle(s, m, blk):
    for at in range(0, blk, 128):
        cs = slice(at, at + 128)
        u = s.db[m, :, cs]
        vhat = s.vh2[m, :, cs]
        add_to(s, AG2, m + at, u * vhat)
        add_to(s, AC2, m + at, u)
        back = norm_back(u, vhat, s.rs2[m, 0:1, cs], s.col[OG2 : OG2 + D].astype(F32))
        dy = s.gt[m, :, cs].astype(F32) + back
        s.db[m, :, cs] = dy
        add_to(s, ABO, m + at, dy)
        s.zb[m % 2, D:, cs] = dy.astype(BF16)
    dp = s.zb[m % 2, D:, :]
    gwo = dot_t(s.ot[m], dp)
    s.ga[:, 3 * D :] = gwo if m == 0 else s.ga[:, 3 * D :] + gwo
    s.bt[m, 0:D, :] = dot_n(s.wo[...], dp).astype(BF16)


def back_attend(s, mb, blk, extra):
    half = blk // 2
    scale = HD ** (-0.5)

    def pre(i):
        m, part, pair, qs, pc = unit_of(i, blk)
        s.hs[i % 2, 0:half, :] = dot_n(s.vn[m, qs, pc], pair_blocks(s.bt[m, pc, qs]))

    def mid(i):
        m, part, pair, qs, pc = unit_of(i, blk)
        for at in range(0, blk, 128):
            head, cs = at // half, slice(at % half, at % half + 128)
            prob = s.prob[m, part, 2 * pair + head, :, cs].astype(F32)
            weighted = prob * s.hs[i % 2, 0:half, at : at + 128]
            ds = weighted - prob * jnp.sum(weighted, axis=0, keepdims=True)
            s.zb[i % 2, 0:half, at : at + 128] = ds.astype(BF16)

    def post(i):
        m, part, pair, qs, pc = unit_of(i, blk)
        for head in range(2):
            hr = slice(pc.start + head * HD, pc.start + head * HD + HD)
            ds = s.zb[i % 2, 0:half, head * half : (head + 1) * half]
            dq = dot_n(s.kt[m, hr, qs], ds) * scale
            dk = dot_t(s.qt[m, hr, qs], ds)
            dv = dot_t(s.bt[m, hr, qs], s.prob[m, part, 2 * pair + head])
            for c, value in enumerate((dq, dk, dv)):
                s.dqkv[m % 2, c * D + hr.start : c * D + hr.stop, qs] = value.astype(BF16)

    pipeline(mb * 2 * PAIRS, pre, mid, post, extra)


def back_grads(s, m, blk):
    g = dot_t(s.at[m], s.dqkv[m % 2])
    s.ga[:, 0 : 3 * D] = g if m == 0 else s.ga[:, 0 : 3 * D] + g
    for at in range(0, blk, 128):
        cs = slice(at, at + 128)
        add_to(s, ABQ, m + at, s.dqkv[m % 2, 0:D, cs].astype(F32))
        add_to(s, ABV, m + at, s.dqkv[m % 2, 2 * D :, cs].astype(F32))


def back_sums(s, m, blk):
    s.dz[m % 2, 0:D, :] = dot_n(s.wcat[...], s.dqkv[m % 2])
    for at in range(0, blk, 128):
        u = s.dz[m % 2, 0:D, at : at + 128]
        add_to(s, AG1, m + at, u * s.vh1[m, :, at : at + 128])
        add_to(s, AC1, m + at, u)


def back_rows(s, m, seg_ref, out_ref, dx_ref, blk):
    for at in range(0, blk, 128):
        cs = slice(at, at + 128)
        u = s.dz[m % 2, 0:D, cs]
        vhat = s.vh1[m, :, cs]
        back = norm_back(u, vhat, s.rs1[m, 0:1, cs], s.col[OG1 : OG1 + D].astype(F32))
        s.dh[m % 2, D:, cs] = (s.db[m, :, cs] + back).astype(BF16)
        s.dh[m % 2, 0:D, cs] = s.out[m, :, cs].astype(BF16)
    start = start_of(seg_ref[m : m + 1, :])
    diff = iota((blk, blk), 0) - iota((blk, blk), 1)
    perm = one_hot((diff == start) | (diff == start - blk))
    both = dot_t(perm, s.dh[m % 2]).astype(BF16)
    out_ref[m * blk : (m + 1) * blk, :] = both[:, 0:D]
    dx_ref[m * blk : (m + 1) * blk, :] = both[:, D:]


def vector_row(s):
    ones = jnp.ones((16, 128), BF16)
    rows = []
    for which in range(8):
        v = s.acc[which]
        high = v.astype(BF16)
        low = (v - high.astype(F32)).astype(BF16)
        rows.append((dot_t(ones, high) + dot_t(ones, low))[0:8, :])
    return jnp.concatenate(rows + [s.g1[D : D + 8, :]], axis=1)


class Names:
    def __init__(self, keys, refs):
        for key, ref in zip(keys, refs):
            setattr(self, key, ref)


class Place:
    def __init__(self):
        wide = lax.axis_index("wide")
        narrow = lax.axis_index("narrow")
        self.z, self.y = lax.div(wide, 2), lax.rem(wide, 2)
        self.x, self.core = lax.div(narrow, 2), lax.rem(narrow, 2)

    def along(self, kind, k):
        if kind == "z":
            z = lax.rem(self.z + k, 4)
            return z, (z * 2 + self.y, self.x * 2 + self.core)
        x = self.x + (k % 2) * (1 - 2 * self.x)
        y = self.y + (k // 2) * (1 - 2 * self.y)
        return y * 2 + x, (self.z * 2 + y, x * 2 + self.core)

    def sibling(self):
        return (self.z * 2 + self.y, self.x * 2 + 1 - self.core)


def device_at(z, plane, core):
    return z * 8 + plane * 2 + core


def slot_of(device):
    return device % 2 * 16 + device // 2 % 4 * 4 + device // 8


def remote(src, dst, send, recv, device):
    return pltpu.make_async_remote_copy(
        src_ref=src, dst_ref=dst, send_sem=send, recv_sem=recv, device_id=device, device_id_type=MESH
    )


def greet(place):
    barrier = pltpu.get_barrier_semaphore()
    partners = [place.along(kind, k)[1] for kind in ("z", "plane") for k in (1, 2, 3)]
    partners.append(place.sibling())
    for partner in partners:
        pl.semaphore_signal(barrier, inc=1, device_id=partner, device_id_type=MESH)
    pl.semaphore_wait(barrier, len(partners))


class Gather:
    def __init__(self, place, whole, parts, send, recv):
        base = place.core * 16
        self.own = base + place.along("plane", 0)[0] * 4 + place.z
        n = len(parts)

        def copy(at, number, to):
            return remote(at, at, send.at[number], recv.at[number], to)

        def part_of(plane, part):
            return part(base + plane * 4)

        self.first = [
            copy(whole(self.own), k - 1, place.along("z", k)[1]) for k in (1, 2, 3)
        ]
        self.second, self.third = [], []
        for p, part in enumerate(parts):
            mine = part_of(place.along("plane", 0)[0], part)
            self.second.append(
                [copy(mine, 2 + 3 * p + k, place.along("plane", k)[1]) for k in (1, 2, 3)]
            )
            self.third.append(
                [
                    copy(
                        part_of(place.along("plane", k)[0], part),
                        3 + 3 * n + 4 * p + k,
                        place.sibling(),
                    )
                    for k in range(4)
                ]
            )

    def start_first(self):
        for copy in self.first:
            copy.start()

    def arrive_first(self):
        for copy in self.first:
            copy.wait_recv()

    def start_second(self, part):
        for copy in self.second[part]:
            copy.start()
        self.third[part][0].start()

    def start_third(self, part):
        for copy, after in zip(self.second[part], self.third[part][1:]):
            copy.wait_recv()
            after.start()

    def finish(self, part):
        for copy in self.third[part]:
            copy.wait_recv()

    def close(self):
        for copy in sum(self.second + self.third, self.first):
            copy.wait_send()


class FastGather:
    def __init__(self, place, buf, send, recv):
        base = place.core * 16
        group = base + place.along("plane", 0)[0] * 4
        self.own = group + place.z

        def copy(at, number, to):
            return remote(at, at, send.at[number], recv.at[number], to)

        self.first = [
            copy(buf.at[self.own], k - 1, place.along("z", k)[1]) for k in (1, 2, 3)
        ]
        self.second = []
        for k in range(4):
            at = buf.at[group + place.along("z", (4 - k) % 4)[0]]
            self.second.append(
                [copy(at, 2 + 3 * k + j, place.along("plane", j)[1]) for j in (1, 2, 3)]
            )
        self.third = [
            copy(
                buf.at[pl.ds(base + place.along("plane", k)[0] * 4, 4)], 15 + k, place.sibling()
            )
            for k in range(4)
        ]

    def start_first(self):
        for copy in self.first + self.second[0]:
            copy.start()

    def start_second(self):
        for k in (1, 2, 3):
            self.first[k - 1].wait_recv()
            for copy in self.second[k]:
                copy.start()
        self.third[0].start()

    def start_third(self):
        for j in (1, 2, 3):
            for k in range(4):
                self.second[k][j - 1].wait_recv()
            self.third[j].start()

    def finish(self):
        for copy in self.third:
            copy.wait_recv()
        for copy in sum(self.second, self.first) + self.third:
            copy.wait_send()


class Scatter:
    def __init__(self, place, line, own, done, buf, got, held, send, recv):
        self.place, self.line, self.own, self.done = place, line, own, done
        self.buf, self.got, self.held = buf, got, held
        n = len(line)
        self.first, self.second, self.third = [], [], []
        for k in range(4):
            at = pl.ds(place.along("plane", k)[0] * n, n)
            self.first.append(
                remote(buf.at[at], got.at[at], send.at[k], recv.at[k], place.sibling())
            )
        for k in (1, 2, 3):
            at = pl.ds((3 + k) * n, n)
            to = place.along("plane", k)[1]
            self.second.append(
                remote(buf.at[at], got.at[at], send.at[3 + k], recv.at[3 + k], to)
            )
            at = 7 * n + k - 1
            to = place.along("z", k)[1]
            self.third.append(
                remote(buf.at[at], got.at[at], send.at[6 + k], recv.at[6 + k], to)
            )

    def owned(self, z, call):
        if len(self.line) == 4:
            call()
        else:
            pl.when((z >= self.line[0]) & (z <= self.line[-1]))(call)

    def start_first(self):
        n = len(self.line)
        for plane in range(4):
            for j, z in enumerate(self.line):
                term = self.own(device_at(z, plane, 1 - self.place.core))
                self.buf[plane * n + j] = term.astype(BF16)
        for k in (3, 1, 2, 0):
            self.first[k].start()

    def start_second(self):
        n = len(self.line)
        for k in (3, 1, 2, 0):
            self.first[k].wait_recv()
            plane = self.place.along("plane", k)[0]
            for j, z in enumerate(self.line):
                term = self.own(device_at(z, plane, self.place.core))
                term = term + self.got[plane * n + j].astype(F32)
                if k == 0:
                    self.held[j] = term
                else:
                    self.buf[(3 + k) * n + j] = term.astype(BF16)
            if k > 0:
                self.second[k - 1].start()

    def start_third(self):
        n = len(self.line)
        for copy in self.second:
            copy.wait_recv()
        for j in range(n):
            term = self.held[j]
            for k in (1, 2, 3):
                term = term + self.got[(3 + k) * n + j].astype(F32)
            self.held[j] = term
        for k in (1, 2, 3):
            z = self.place.along("z", k)[0]

            def send(k=k, z=z):
                self.buf[7 * n + k - 1] = self.held[z - self.line[0]].astype(BF16)
                self.third[k - 1].start()

            self.owned(z, send)

    def finish(self):
        n = len(self.line)

        def take():
            term = self.held[self.place.z - self.line[0]]
            for k in (1, 2, 3):
                self.third[k - 1].wait_recv()
                term = term + self.got[7 * n + k - 1].astype(F32)
            self.done(term)

        self.owned(self.place.z, take)
        for copy in self.first + self.second:
            copy.wait_send()
        for k in (1, 2, 3):
            self.owned(self.place.along("z", k)[0], self.third[k - 1].wait_send)


def entry_place(k):
    gain, rest = k < 512.0, k - 512.0
    device = jnp.where(gain, jnp.floor((k + 0.5) * (1.0 / 16)), jnp.floor((rest + 0.5) * (1.0 / 112)))
    lane = jnp.where(gain, k - 16.0 * device, rest - 112.0 * device + 16.0)
    return device, lane


def pick_at(s, at):
    ref = s.w1t if at < FF else s.w2
    return ref.at[at % FF : at % FF + 512]


def make_tables(s):
    row = iota((8, 256), 1)
    slot = row // 8
    device = slot % 4 * 8 + slot // 4 % 4 * 2 + slot // 16
    first_gain = jnp.where(row % 8 == 0, 16 * device, 8192)[0:1, :]
    first_bias = jnp.where(row % 8 == 0, 512 + 112 * device, 8192)[0:1, :]
    for at in range(0, NVEC, 512):
        k = iota((512, 256), 0) + at
        first, count = (first_gain, 16) if at < 512 else (first_bias, 112)
        pick_at(s, at)[...] = one_hot((k >= first) & (k < first + count))
        _, lane = entry_place((iota((512, 128), 0) + at).astype(F32))
        s.keep[at : at + 512, :] = one_hot(lane == iota((512, 128), 1).astype(F32))
    device, _ = entry_place(iota((16, NVEC), 1).astype(F32))
    for at in (0, 16):
        s.mine[at : at + 16, :] = one_hot(device == (iota((16, NVEC), 0) + at).astype(F32))


def unpack_attention(s):
    for c in range(4):
        rows = [s.bufa[slot_of(d), 8 * c : 8 * c + 8, :].astype(F32) for d in range(32)]
        full = jnp.concatenate(rows, axis=0).astype(BF16)
        if c < 3:
            s.wcat[:, c * D : (c + 1) * D] = full
        else:
            s.wo[...] = full
    unpack_vectors(s, range(0, OB1, 512))


def unpack_vectors(s, blocks):
    rows = [s.bufa[d, 32:40, 0:128].astype(F32) for d in range(32)]
    table = jnp.concatenate(rows, axis=0).astype(BF16)
    ones = jnp.ones((128, 128), BF16)
    for at in blocks:
        found = dot_n(pick_at(s, at)[...], table).astype(BF16) * s.keep[at : at + 512, :]
        s.col[at : at + 512, :] = dot_n(found, ones).astype(BF16)


def unpack_inner(s, part):
    for i in range(16):
        pair = [s.buf1[part, slot_of(2 * i + c)].astype(F32) for c in range(2)]
        for h in range(2):
            rows = jnp.concatenate([v[8 * h : 8 * h + 8] for v in pair], axis=0)
            at = part * (FF // 4) + h * D
            s.w1[16 * i : 16 * i + 16, at : at + D] = rows.astype(BF16)
    for d in range(8 * part, 8 * part + 8):
        s.w2[64 * d : 64 * d + 64, :] = s.buf2[slot_of(d)]
    transpose_weights_inner(s, (2 * part, 2 * part + 1))


def vector_rows(s):
    row = vector_row(s)[0:1, :]
    high = row.astype(BF16).astype(F32)
    total = None
    for term in (high, row - high):
        part = dot_n((s.mine[...].astype(F32) * term).astype(BF16), s.keep[...])
        total = part if total is None else total + part
    high = total.astype(BF16).astype(F32)
    s.vrow[:, 0:128] = high
    s.vrow[:, 128:256] = total - high


def fold(rows):
    half = rows.shape[1] // 2
    return jnp.concatenate([rows[:, :half], rows[:, half:]], axis=0)


def own_attention(s, cols):
    return lambda device: fold(s.ga[pl.ds(pl.multiple_of(device * 8, 8), 8), cols])


def own_vector(s):
    return lambda device: fold(jnp.broadcast_to(s.vrow[pl.ds(device, 1), :], (8, D)))


def own_first(s, half):
    cols = slice(half * (FF // 2), (half + 1) * (FF // 2))
    return lambda device: fold(s.g1[pl.ds(pl.multiple_of(device * 8, 8), 8), cols])


def own_second(s):
    return lambda device: s.g2[pl.ds(pl.multiple_of(device * 64, 64), 64), :]


MSG = 40
SUMS = {
    "q": (4, 16, 3 * D // 2),
    "o": (4, 16, D // 2),
    "v": (4, 16, D // 2),
    "1x": (4, 16, FF // 4),
    "1y": (4, 16, FF // 4),
    "2x": (2, 64, D),
    "2y": (2, 64, D),
}


def fused_scratch(mb, blk):
    shapes = scratch_shapes(mb, blk)
    for name, (rows, cols) in (("a", (MSG, D)), ("1", (16, FF // 8)), ("2", (64, D))):
        lead = (4, 32) if name == "1" else (32,)
        shapes["buf" + name] = pltpu.VMEM((*lead, rows, cols), BF16)
        shapes["gsend" + name] = pltpu.SemaphoreType.DMA((24,))
        shapes["grecv" + name] = pltpu.SemaphoreType.DMA((24,))
    for name, (n, rows, cols) in SUMS.items():
        if name != "2x":
            shapes["out" + name] = pltpu.VMEM((7 * n + 3, rows, cols), BF16)
        shapes["got" + name] = pltpu.VMEM((7 * n + 3, rows, cols), BF16)
        shapes["held" + name] = pltpu.VMEM((n, rows, cols), F32)
        shapes["ssend" + name] = pltpu.SemaphoreType.DMA((10,))
        shapes["srecv" + name] = pltpu.SemaphoreType.DMA((10,))
    shapes["keep"] = pltpu.VMEM((NVEC, 128), BF16)
    shapes["mine"] = pltpu.VMEM((32, NVEC), BF16)
    shapes["vrow"] = pltpu.VMEM((32, D), F32)
    shapes["line"] = pltpu.VMEM((8, D), F32)
    for name in ("xs", "gs"):
        shapes[name] = pltpu.VMEM((mb * blk, D), BF16)
    shapes["insem"] = pltpu.SemaphoreType.DMA((2,))
    shapes["outsem"] = pltpu.SemaphoreType.DMA((2 * mb,))
    return shapes


def fused_kernel(keys, mb, blk, *refs):
    x_hbm, seg_ref, g_hbm, wa, w1, w2, gains, biases = refs[:8]
    out_hbm, dx_hbm, sumq, sumo, sumv, sum1, sum2 = refs[8:15]
    s = Names(keys, refs[15:])
    place = Place()
    loads = []
    for i, (hbm, ref) in enumerate(((x_hbm, s.xs), (g_hbm, s.gs))):
        loads.append(pltpu.make_async_copy(hbm, ref, s.insem.at[i]))
        loads[-1].start()
    refs = {n: [getattr(s, key + n) for key in ("buf", "gsend", "grecv")] for n in "a12"}
    gather = {
        "a": FastGather(place, *refs["a"]),
        "1": Gather(
            place,
            lambda slot: s.buf1.at[:, slot],
            [lambda at, p=p: s.buf1.at[p, pl.ds(at, 4)] for p in (0, 1, slice(2, 4))],
            *refs["1"][1:],
        ),
        "2": Gather(
            place,
            lambda slot: s.buf2.at[slot],
            [lambda at, z=z: s.buf2.at[pl.ds(at + z, (z + 2) // 2)] for z in range(3)],
            *refs["2"][1:],
        ),
    }
    s.line[...] = jnp.zeros((8, D), F32)
    s.line[0:1, 0:16] = gains[...]
    s.line[0:1, 16:128] = biases[...]
    own = jnp.concatenate([wa[c] for c in range(4)] + [s.line[...]], axis=0).astype(BF16)
    s.bufa[gather["a"].own] = own
    greet(place)
    gather["a"].start_first()
    for p in range(4):
        cols = fold(w1[:, p * (FF // 4) : (p + 1) * (FF // 4)])
        s.buf1[p, gather["1"].own] = cols.astype(BF16)
    s.buf2[gather["2"].own] = w2[...].astype(BF16)
    gather["1"].start_first()
    gather["2"].start_first()
    make_tables(s)
    gather["a"].start_second()
    for copy in loads:
        copy.wait()
    for m in range(mb):
        load_rows(s, m, s.xs, s.gs, seg_ref, blk)
    gather["a"].start_third()
    for n in "12":
        gather[n].arrive_first()
    for part in range(3):
        for n in "12":
            gather[n].start_second(part)
    gather["a"].finish()
    unpack_attention(s)
    transpose_weights_attention(s)
    project(s, 0, blk)
    extra = {}

    def at(step, f, *args):
        extra.setdefault(step, []).append(functools.partial(f, *args))

    for m in range(mb):
        if m + 1 < mb:
            at(4 * m + 1, project, s, m + 1, blk)
        at(4 * m + 4, middle, s, m, blk)
    for n in "12":
        at(8, gather[n].start_third, 0)
        at(14, gather[n].start_third, 1)
    at(7, unpack_vectors, s, range(OB1, NVEC, 512))
    attend(s, mb, blk, extra)
    for n in "12":
        gather[n].finish(0)
    unpack_inner(s, 0)
    scatter = {}
    s.out2x = s.buf2.at[0:17]

    def sum_into(name, line, own, done):
        refs = [getattr(s, key + name) for key in ("out", "got", "held", "ssend", "srecv")]
        scatter[name] = Scatter(place, line, own, done, *refs)

    def into(ref):
        def store(value):
            ref[...] = value

        return store

    def into_first(half):
        def store(value):
            for part in range(2):
                at = (2 * half + part) * FF // 4
                sum1[:, at : at + FF // 4] = value[8 * part : 8 * part + 8]

        return store

    sum_into("q", range(4), own_attention(s, slice(0, 3 * D)), into(sumq))
    sum_into("o", range(4), own_attention(s, slice(3 * D, 4 * D)), into(sumo))
    sum_into("v", range(4), own_vector(s), into(sumv))
    for half, name in enumerate("xy"):
        sum_into("1" + name, range(4), own_first(s, half), into_first(half))
        sum_into("2" + name, range(2 * half, 2 * half + 2), own_second(s), into(sum2))
    feed_forward(s, mb, blk, first=0, last=1, limit=1)
    for n in "12":
        gather[n].finish(1)
        gather[n].start_third(2)
    unpack_inner(s, 1)
    feed_forward(s, mb, blk, first=1, last=2, limit=2)
    for n in "12":
        gather[n].finish(2)
        gather[n].close()
    unpack_inner(s, 2)
    unpack_inner(s, 3)
    scatter["1x"].start_first()
    scatter["2x"].start_first()
    later = [(2, scatter[n].start_second) for n in ("1x", "2x")]
    feed_forward(s, mb, blk, first=2, last=3, hooks=later)
    feed_forward(s, mb, blk, first=3, last=4, lead=False)
    scatter["1y"].start_first()
    scatter["2y"].start_first()
    saves = []

    def last_rows(m):
        back_rows(s, m, seg_ref, s.xs, s.gs, blk)
        rows = pl.ds(m * blk, blk)
        for kind, (ref, hbm) in enumerate(((s.xs, out_hbm), (s.gs, dx_hbm))):
            sem = s.outsem.at[2 * m + kind]
            saves.append(pltpu.make_async_copy(ref.at[rows], hbm.at[rows], sem))
            saves[-1].start()

    back_middle(s, 0, blk)
    extra.clear()
    for m in range(mb):
        if m + 1 < mb:
            at(4 * m + 1, back_middle, s, m + 1, blk)
        at(4 * m + 4, back_grads, s, m, blk)
        if m + 2 < mb:
            at(4 * m + 5, back_sums, s, m, blk)
            at(4 * m + 5, last_rows, m)
    for n in "12":
        at(3, scatter[n + "x"].start_third)
        at(2, scatter[n + "y"].start_second)
        at(12, scatter[n + "x"].finish)
        at(14, scatter[n + "y"].start_third)
    at(11, scatter["o"].start_first)
    at(13, scatter["o"].start_second)
    back_attend(s, mb, blk, extra)
    scatter["q"].start_first()
    back_sums(s, mb - 2, blk)
    back_sums(s, mb - 1, blk)
    vector_rows(s)
    scatter["v"].start_first()
    scatter["q"].start_second()
    scatter["v"].start_second()
    scatter["o"].start_third()
    last_rows(mb - 2)
    last_rows(mb - 1)
    scatter["1y"].finish()
    scatter["2y"].finish()
    scatter["q"].start_third()
    scatter["v"].start_third()
    scatter["o"].finish()
    for copy in saves:
        copy.wait()
    scatter["q"].finish()
    scatter["v"].finish()


STEP = 10
BETA_ONE = 0.9
BETA_TWO = 0.999
ADAM_EPS = 1e-08
RATES = (0.08, 0.08, 0.08, 0.6, 0.6)
DECAYS = (0.01, 0.01, 0.01, 0.0, 0.0)


def adamw(weight, grad, first, second, rate, decay):
    first_new = BETA_ONE * first + (1.0 - BETA_ONE) * grad
    second_new = BETA_TWO * second + (1.0 - BETA_TWO) * grad * grad
    first_hat = first_new / (1.0 - BETA_ONE**STEP)
    second_hat = second_new / (1.0 - BETA_TWO**STEP)
    weight_new = weight - rate * (first_hat / (jnp.sqrt(second_hat) + ADAM_EPS) + decay * weight)
    return weight_new, first_new, second_new


def adam_kernel(*refs):
    sumq, sumo, sumv, sum1, sum2 = refs[:5]
    state, rows, new, saved, sem = refs[5:20], refs[20:22], refs[22:37], refs[37:39], refs[39]
    copies = [pltpu.make_async_copy(rows[i], saved[i], sem.at[i]) for i in range(2)]
    for copy in copies:
        copy.start()

    def update(member, grad, at=()):
        at = at if at else (slice(None),)
        values = adamw(
            state[member][at], grad, state[5 + member][at], state[10 + member][at], RATES[member], DECAYS[member]
        )
        for kind in range(3):
            new[5 * kind + member][at] = values[kind]

    grads = jnp.concatenate([sumq[0:8, :], sumq[8:16, :], sumo[0:8, :], sumo[8:16, :]], axis=1)
    for c in range(4):
        update(0, grads[:, c * D : (c + 1) * D], (c,))
    update(1, sum1[...])
    update(2, sum2[...])
    line = sumv[0:1, :] + sumv[8:9, :]
    update(3, line[:, 0:16])
    update(4, line[:, 16:128])
    for copy in copies:
        copy.wait()


VMEM_SPEC = pl.BlockSpec(memory_space=pltpu.VMEM)
ANY_SPEC = pl.BlockSpec(memory_space=pl.ANY)


def fused_device(*args):
    frames, segments, out_grad = args[:3]
    rows = lambda v: v.reshape(1, -1) if v.ndim == 1 else v
    state = [rows(v) for v in args[3:]]
    mb, blk = segments.shape
    shapes = fused_scratch(mb, blk)
    like = lambda v: jax.ShapeDtypeStruct(v.shape, v.dtype)
    out, dx, *sums = pl.pallas_call(
        functools.partial(fused_kernel, list(shapes), mb, blk),
        out_shape=[like(frames), like(frames)]
        + [jax.ShapeDtypeStruct(t, F32) for t in ((16, 3 * D // 2), (16, D // 2), (16, D // 2), (8, FF), (64, D))],
        in_specs=[ANY_SPEC, VMEM_SPEC, ANY_SPEC] + [VMEM_SPEC] * 5,
        out_specs=[ANY_SPEC] * 2 + [VMEM_SPEC] * 5,
        scratch_shapes=list(shapes.values()),
        compiler_params=pltpu.CompilerParams(
            collective_id=0, has_side_effects=True, vmem_limit_bytes=63 * 2**20
        ),
    )(frames, segments, out_grad, *state[:5])
    *new, out, dx = pl.pallas_call(
        adam_kernel,
        out_shape=[like(v) for v in state] + [like(out), like(dx)],
        in_specs=[VMEM_SPEC] * 22,
        out_specs=[VMEM_SPEC] * 15 + [ANY_SPEC] * 2,
        scratch_shapes=[pltpu.SemaphoreType.DMA((2,))],
    )(*sums, *state, out, dx)
    return (out, dx, *[v.reshape(t.shape) for v, t in zip(new, args[3:])])


def local_kernel(keys, mb, blk, *refs):
    x_ref, seg_ref, g_ref, wa, w1, w2, col = refs[:7]
    out_ref, dx_ref, ga, g1, g2, gv = refs[7:13]
    s = Names(keys, refs[13:])
    for c in range(3):
        s.wcat[:, c * D : (c + 1) * D] = wa[c]
    s.wo[...] = wa[3]
    s.w1[...] = w1[...]
    s.w2[...] = w2[...]
    s.col[...] = col[...].astype(BF16)
    transpose_weights_attention(s)
    transpose_weights_inner(s, range(FF // D))
    for m in range(mb):
        load_rows(s, m, x_ref, g_ref, seg_ref, blk)
        project(s, m, blk)
    attend(s, mb, blk, {})
    for m in range(mb):
        middle(s, m, blk)
    feed_forward(s, mb, blk)
    extra = {}
    for m in range(mb):
        back_middle(s, m, blk)
        extra[4 * m + 4] = [
            functools.partial(back_grads, s, m, blk),
            functools.partial(back_sums, s, m, blk),
            functools.partial(back_rows, s, m, seg_ref, out_ref, dx_ref, blk),
        ]
    back_attend(s, mb, blk, extra)
    gv[...] = vector_row(s)
    ga[...] = s.ga[...]
    g1[...] = s.g1[0:D, :]
    g2[...] = s.g2[...]


AXES = ("wide", "narrow")


def local_device(*args):
    frames, segments, out_grad = args[:3]
    weights, firsts, seconds = args[3:8], args[8:13], args[13:18]
    dims = (1, 0, 0, 0, 0)
    full = [
        lax.all_gather(w.astype(BF16), AXES, axis=dim, tiled=True) for w, dim in zip(weights, dims)
    ]
    mb, blk = segments.shape
    table = jnp.concatenate([full[3], full[4]]).astype(F32)
    shapes = scratch_shapes(mb, blk)
    like = lambda v: jax.ShapeDtypeStruct(v.shape, v.dtype)
    out, dx, ga, g1, g2, gv = pl.pallas_call(
        functools.partial(local_kernel, list(shapes), mb, blk),
        out_shape=[like(frames), like(frames)]
        + [jax.ShapeDtypeStruct(t, F32) for t in ((D, 4 * D), (D, FF), (FF, D), (8, NVEC))],
        in_specs=[VMEM_SPEC] * 7,
        out_specs=[VMEM_SPEC] * 6,
        scratch_shapes=list(shapes.values()),
        compiler_params=pltpu.CompilerParams(vmem_limit_bytes=63 * 2**20),
    )(frames, segments, out_grad, *full[:3], jnp.broadcast_to(table[:, None], (NVEC, 128)))
    grads = (jnp.stack(jnp.split(ga, 4, axis=1)), g1, g2, gv[0, :512], gv[0, 512:])
    owned = [
        lax.psum_scatter(g, AXES, scatter_dimension=dim, tiled=True) for g, dim in zip(grads, dims)
    ]
    new = [adamw(*v) for v in zip(weights, owned, firsts, seconds, RATES, DECAYS)]
    return (out, dx, *[new[member][kind] for kind in range(3) for member in range(5)])


def solution(mesh):
    rows, matrix, vector = P(AXES, None), P(None, AXES, None), P(AXES)
    group = (matrix, rows, rows, vector, vector)
    fits = (mesh.shape["wide"], mesh.shape["narrow"]) == (8, 4)
    return jax.shard_map(
        fused_device if fits else local_device,
        mesh=mesh,
        in_specs=(rows, rows, rows, *group, *group, *group),
        out_specs=(rows, rows, *group, *group, *group),
        check_vma=False,
    )
```
